128 devices in a mesh: dp: 32 (over z, y, core), mp: 4 (over x).
Axes of the slice: x: 4, y: 4, z: 4, core: 2. Of those that a mesh axis runs over, the one named last changes fastest.
Arguments:
- gradients: bfloat16 [32, 4, 28, 512, 512], P('dp', 'mp'), may hold values from -24 to 24
- left_stats: float32 [4, 64, 512, 512], P('mp', 'dp'), may hold values from -1 to 4, as said below
- right_stats: float32 [4, 64, 512, 512], P('mp', 'dp'), may hold values from -1 to 4, as said below
- owner_list: int32 [4, 28], replicated, may hold values from 0 to 31, as said below
- owner_counts: int32 [4, 32], replicated, may hold values from 0 to 2, as said below
- block_offsets: int32 [4, 32], replicated, may hold values from 0 to 28, as said below
Outputs:
- new_left: float32 [4, 64, 512, 512], P('mp', 'dp')
- new_right: float32 [4, 64, 512, 512], P('mp', 'dp')
- update: bfloat16 [4, 28, 512, 512], P(None, None, 'dp')
The draws below stay inside these ranges and needn't reach their ends.
Inputs may be any that keep to these rules, and one draw needn't show every extreme that they name: Each owner's blocks are consecutive: block_offsets[g, o] is the sum of owner_counts[g, p] over p < o, and owner_list[g, k] = o exactly for the blocks block_offsets[g, o] .. block_offsets[g, o] + owner_counts[g, o] - 1. The counts of a group sum to 28; some owner of every group holds 2. `block_offsets`: consistent with owner_counts as stated there. `owner_list`: consistent with owner_counts as stated there. `left_stats`: symmetric positive definite. `right_stats`: symmetric positive definite.
All inputs are finite; a program needn't handle non-finite values. Where the reference program divides by a largest or mean magnitude, that divisor is 1e-20 or more.
Results may differ from the reference program's by a relative error of at most 0.015.
Values may be sent and summed in bfloat16 or wider, within the bound.
No kernel may reach another device: no remote copies, remote signals or barrier semaphores. Data moves between devices by JAX's collectives and lax.ppermute only.
A program may use at most 192 MiB of HBM per device.

```python
import math
import jax
import jax.numpy as jnp
from jax import lax

B = 512
SLOTS = 2
ITERS = 3
OWNERS = 32
GROUPS = 4
NBLK = 28


def owner_plan(key):

    def plan_group(group_key):
        key_count, key_order = jax.random.split(group_key)
        doubled = jax.random.randint(key_count, (), 1, NBLK // 2 + 1)
        shuffled = jax.random.permutation(key_order, OWNERS)
        ranking = jnp.argsort(shuffled)
        counts = jnp.where(ranking < doubled, SLOTS, jnp.where(ranking < NBLK - doubled, 1, 0)).astype(jnp.int32)
        offsets = (jnp.cumsum(counts) - counts).astype(jnp.int32)
        block_ends = offsets + counts
        block_ids = jnp.arange(NBLK, dtype=jnp.int32)
        owners = jnp.sum((block_ends[None, :] <= block_ids[:, None]).astype(jnp.int32), axis=1)
        return (owners.astype(jnp.int32), counts, offsets)
    return jax.vmap(plan_group)(jax.random.split(key, GROUPS))


def draw_owner_list(key, part):
    return owner_plan(key)[0]


def draw_owner_counts(key, part):
    return owner_plan(key)[1]


def draw_block_offsets(key, part):
    return owner_plan(key)[2]


def spd_blocks(key, lowest, highest):
    key_noise, key_diag, key_scale = jax.random.split(key, 3)
    shape = (GROUPS, OWNERS * SLOTS, B, B)
    noise = jax.random.uniform(key_noise, shape, jnp.float32, -1.0, 1.0)
    symmetric = 0.5 * (noise + jnp.swapaxes(noise, -1, -2))
    diagonal = jax.random.uniform(key_diag, (GROUPS, OWNERS * SLOTS, B, 1), jnp.float32, 1.02, 1.5)
    marker = (jnp.arange(B)[:, None] == jnp.arange(B)[None, :]).astype(jnp.float32)
    base = symmetric * (1.0 - marker) + marker * diagonal * (B - 1)
    scales = jnp.exp(jax.random.uniform(key_scale, (GROUPS, OWNERS * SLOTS, B, 1), jnp.float32, math.log(lowest), math.log(highest)))
    return base * scales * jnp.swapaxes(scales, -1, -2) / B


def draw_left_stats(key, part):
    key = jax.random.fold_in(key, 3)
    return spd_blocks(key, 0.12, 1.2)


def draw_right_stats(key, part):
    key = jax.random.fold_in(key, 5)
    return spd_blocks(key, 0.12, 1.2)


def scaled_gradients(key, lowest, highest, own_weight):
    key_row, key_col, key_own = jax.random.split(key, 3)
    rows = jnp.exp(jax.random.uniform(key_row, (1, GROUPS, NBLK, B, 1), jnp.float32, math.log(lowest), math.log(highest)))
    columns = jnp.exp(jax.random.uniform(key_col, (1, GROUPS, NBLK, 1, B), jnp.float32, math.log(lowest), math.log(highest)))
    noise = jax.random.truncated_normal(key_own, -4.0, 4.0, (OWNERS, GROUPS, NBLK, B, B), jnp.float32)
    return (rows, columns, own_weight * noise)


def draw_gradients(key, part):
    key = jax.random.fold_in(key, 11)
    rows, columns, values = scaled_gradients(key, 0.3, 3.0, 0.2)
    return (rows * columns * values).astype(jnp.bfloat16)


def setup_inputs(seed: int = 0) -> dict:
    splits = jax.random.split(jax.random.key(seed), 7)
    return {
        "gradients": draw_gradients(jax.random.fold_in(splits[6], 71), 0),
        "left_stats": draw_left_stats(jax.random.fold_in(splits[6], 71), 0),
        "right_stats": draw_right_stats(jax.random.fold_in(splits[6], 71), 0),
        "owner_list": draw_owner_list(jax.random.fold_in(splits[6], 71), 0),
        "owner_counts": draw_owner_counts(jax.random.fold_in(splits[6], 71), 0),
        "block_offsets": draw_block_offsets(jax.random.fold_in(splits[6], 71), 0),
    }


def matmul(first_mat, second_mat):
    return jnp.dot(first_mat, second_mat, precision=lax.Precision.HIGHEST, preferred_element_type=jnp.float32)

def inverse_root(statistic):
    identity = jnp.eye(B, dtype=jnp.float32)
    scale = jnp.max(lax.optimization_barrier(jnp.sum(jnp.abs(statistic), axis=1))) + 1e-06
    target = statistic / scale
    iterate = identity
    for sweep in range(ITERS):
        factor = (5.0 * identity - target) * 0.25
        iterate = factor if sweep == 0 else matmul(iterate, factor)
        if sweep < ITERS - 1:
            square = matmul(factor, factor)
            target = matmul(square, matmul(square, target))
    return iterate * (1.0 / jnp.sqrt(jnp.sqrt(scale)))

def slot_step(items):
    left, right, block, alive = items
    gram_left = matmul(block, block.T)
    gram_right = matmul(block.T, block)
    fresh_left = jnp.where(alive, 0.9 * left + 0.1 / B * gram_left, left)
    fresh_right = jnp.where(alive, 0.9 * right + 0.1 / B * gram_right, right)
    root_left = inverse_root(fresh_left)
    root_right = inverse_root(fresh_right)
    result = matmul(root_left, matmul(block, root_right)).astype(jnp.bfloat16)
    return (fresh_left, fresh_right, result)

def reference(gradients, left_stats, right_stats, owner_list, owner_counts, block_offsets):
    summed = lax.optimization_barrier(jnp.sum(gradients, axis=0, dtype=jnp.float32))
    slot_ids = jnp.arange(SLOTS, dtype=jnp.int32)
    lefts = []
    rights = []
    updates = []
    for group_id in range(GROUPS):
        counts_row = owner_counts[group_id]
        offsets_row = block_offsets[group_id]
        wanted = jnp.minimum(offsets_row[:, None] + slot_ids[None, :], NBLK - 1).reshape(-1)
        alive = (slot_ids[None, :] < counts_row[:, None]).reshape(-1)
        blocks = summed[group_id][wanted] * alive[:, None, None].astype(summed.dtype)
        fresh_left, fresh_right, slot_updates = lax.map(slot_step, (left_stats[group_id], right_stats[group_id], blocks, alive))
        owners_row = owner_list[group_id]
        position = owners_row * SLOTS + jnp.arange(NBLK, dtype=jnp.int32) - offsets_row[owners_row]
        lefts.append(fresh_left)
        rights.append(fresh_right)
        updates.append(slot_updates[position])
    return (jnp.stack(lefts), jnp.stack(rights), jnp.stack(updates))
```

```python
import jax
import jax.numpy as jnp
import numpy as np
from jax import lax
from jax.experimental import pallas as pl
from jax.experimental.pallas import tpu as pltpu
from jax.sharding import PartitionSpec as P

RING = 4
CORES = 2
START = 25.0 / 16.0


def tail_coefficients():
    m1 = np.polynomial.Polynomial([1.25, -0.25])
    m2 = 1.25 - 0.25 * np.polynomial.Polynomial([0.0, 1.0]) * m1**4
    return [float(v) for v in (m1 * m2).coef]


TAIL = tail_coefficients()
EYE_PART = 1.25 * TAIL[0]


def dot(first, second, dims=((1,), (0,))):
    return lax.dot_general(
        first.astype(jnp.bfloat16),
        second.astype(jnp.bfloat16),
        (dims, ((), ())),
        preferred_element_type=jnp.float32,
    )


def roots(statistics):
    both = range(len(statistics))
    scales = [jnp.max(jnp.sum(jnp.abs(a), axis=0, keepdims=True), axis=1, keepdims=True) + 1e-06 for a in statistics]
    z = [statistics[i] * (1.0 / scales[i]) for i in both]
    zb = [z[i].astype(jnp.bfloat16) for i in both]
    square = [dot(zb[i], zb[i]) for i in both]
    e = [(0.0625 * square[i] - 0.625 * z[i]).astype(jnp.bfloat16) for i in both]
    t = [START * z[i] + dot(e[i], zb[i]) for i in both]
    y = [START * t[i] + dot(e[i], t[i]) for i in both]
    yb = [y[i].astype(jnp.bfloat16) for i in both]
    y2 = [dot(yb[i], yb[i]) for i in both]
    y3 = [dot(y2[i], yb[i]) for i in both]
    y3b = [y3[i].astype(jnp.bfloat16) for i in both]
    high = [(TAIL[6] * y3[i] + TAIL[5] * y2[i] + TAIL[4] * y[i]).astype(jnp.bfloat16) for i in both]
    q = [TAIL[1] * y[i] + TAIL[2] * y2[i] + TAIL[3] * y3[i] + dot(high[i], y3b[i]) for i in both]
    f = [1.25 * q[i] - (0.25 * TAIL[0]) * z[i] - 0.25 * dot(zb[i], q[i]) for i in both]
    return f, [1.0 / jnp.sqrt(jnp.sqrt(s)) for s in scales]


def slot_kernel(count_ref, block_ref, left_ref, right_ref, new_left_ref, new_right_ref, update_ref):
    alive = pl.program_id(0) < count_ref[0]
    extent = left_ref.shape[-1]

    @pl.when(jnp.logical_not(alive))
    def _():
        new_left_ref[...] = left_ref[...]
        new_right_ref[...] = right_ref[...]
        update_ref[...] = jnp.zeros_like(update_ref)

    @pl.when(alive)
    def _():
        block = block_ref[:, 0].reshape(extent, extent)
        fresh_left = 0.9 * left_ref[0] + (0.1 / extent) * dot(block, block, ((1,), (1,)))
        fresh_right = 0.9 * right_ref[0] + (0.1 / extent) * dot(block, block, ((0,), (0,)))
        new_left_ref[0] = fresh_left
        new_right_ref[0] = fresh_right
        (f_left, f_right), (c_left, c_right) = roots([fresh_left, fresh_right])
        half = EYE_PART * block.astype(jnp.float32) + dot(block, f_right)
        result = (EYE_PART * half + dot(f_left, half)) * (c_left * c_right)
        update_ref[:, 0] = result.astype(jnp.bfloat16).reshape(update_ref.shape[0], update_ref.shape[2], extent)


def slot_step(count, received, left, right):
    owners, slots, rows, extent = received.shape
    spread = pl.BlockSpec((owners, 1, rows, extent), lambda s, count: (0, s, 0, 0))
    whole = pl.BlockSpec((1, extent, extent), lambda s, count: (s, 0, 0))
    return pl.pallas_call(
        slot_kernel,
        grid_spec=pltpu.PrefetchScalarGridSpec(
            num_scalar_prefetch=1,
            grid=(slots,),
            in_specs=[spread, whole, whole],
            out_specs=[whole, whole, spread],
        ),
        out_shape=[
            jax.ShapeDtypeStruct(left.shape, jnp.float32),
            jax.ShapeDtypeStruct(right.shape, jnp.float32),
            jax.ShapeDtypeStruct(received.shape, jnp.bfloat16),
        ],
        compiler_params=pltpu.CompilerParams(vmem_limit_bytes=56 * 1024 * 1024),
        cost_estimate=pl.CostEstimate(
            flops=slots * 18 * 2 * extent**3,
            bytes_accessed=4 * left.size * 4 + 2 * received.size * 2,
            transcendentals=0,
        ),
    )(count, received, left, right)


def shifted(axis, steps):
    pairs = []
    for z in range(RING):
        for y in range(RING):
            for core in range(CORES):
                to = [z, y, core]
                to[axis] = (to[axis] + steps) % (CORES if axis == 2 else RING)
                pairs.append(((z * RING + y) * CORES + core, (to[0] * RING + to[1]) * CORES + to[2]))
    return pairs


def send(value, axis, steps):
    return lax.ppermute(value.astype(jnp.bfloat16), "dp", shifted(axis, steps))


def reduce_scatter(gradient, z, y, core):
    blocks, extent = gradient.shape[0], gradient.shape[1]
    rows = extent // (RING * RING * CORES)
    view = gradient.reshape(blocks, RING, RING, CORES, rows, extent)
    part_blocks = blocks // 2
    mid = part_blocks // 2
    f32 = jnp.float32
    where = (z, y)

    def rows_for(part, away, which_core):
        first = 1 - part
        starts = [part * part_blocks, 0, 0, which_core, 0, 0]
        starts[1 + first] = (where[first] + away) % RING
        sizes = [part_blocks, RING, RING, 1, rows, extent]
        sizes[1 + first] = 1
        return lax.dynamic_slice(view, starts, sizes).reshape(part_blocks, RING, rows, extent)

    chip = {}
    for away in (2, 1, 3, 0):
        for part in (0, 1):
            other = send(rows_for(part, away, 1 - core), 2, 1)
            chip[part, away] = rows_for(part, away, core).astype(f32) + other.astype(f32)
    ahead, back = {}, {}
    for part in (0, 1):
        ahead[part] = send(chip[part, 2][:mid], 1 - part, 1)
        back[part] = send(chip[part, 2][mid:], 1 - part, -1)
    ahead_raw, back_raw = {}, {}
    for part in (0, 1):
        ahead_raw[part] = send(chip[part, 1][mid:], 1 - part, 1)
        back_raw[part] = send(chip[part, 3][:mid], 1 - part, -1)
    ahead_sum, back_sum = {}, {}
    for part in (0, 1):
        ahead_sum[part] = send(chip[part, 1][:mid] + ahead[part].astype(f32), 1 - part, 1)
        back_sum[part] = send(chip[part, 3][mid:] + back[part].astype(f32), 1 - part, -1)
    results = []
    for part in (0, 1):
        own = chip[part, 0]
        low = own[:mid] + ahead_sum[part].astype(f32) + back_raw[part].astype(f32)
        top = own[mid:] + ahead_raw[part].astype(f32) + back_sum[part].astype(f32)
        line = jnp.concatenate([low, top], 0)
        second = part

        def piece(away):
            return lax.dynamic_index_in_dim(line, (where[second] + away) % RING, 1, keepdims=False)

        arrived = [send(piece(away), second, away) for away in (1, 3, 2)]
        total = piece(0)
        for value in arrived:
            total = total + value.astype(f32)
        results.append(total.astype(jnp.bfloat16))
    return jnp.concatenate(results, 0)


def gather_groups(mine, group):
    count = lax.axis_size("mp")
    up = [(i, (i + 1) % count) for i in range(count)]
    down = [(i, (i - 1) % count) for i in range(count)]
    mid = mine.shape[0] // 2
    low, top = mine[:mid], mine[mid:]
    below_low = lax.ppermute(low, "mp", up)
    above_top = lax.ppermute(top, "mp", down)
    below_top = lax.ppermute(top, "mp", up)
    above_low = lax.ppermute(low, "mp", down)
    far_low = lax.ppermute(below_low, "mp", up)
    far_top = lax.ppermute(above_top, "mp", down)
    out = jnp.zeros((count,) + mine.shape, mine.dtype)
    for away, part, value in (
        (0, 0, low),
        (0, mid, top),
        (-1, 0, below_low),
        (-1, mid, below_top),
        (1, 0, above_low),
        (1, mid, above_top),
        (2, 0, far_low),
        (2, mid, far_top),
    ):
        out = lax.dynamic_update_slice(out, value[None], ((group + away) % count, part, 0, 0))
    return out


def per_device(gradients, left_stats, right_stats, owner_list, owner_counts, block_offsets):
    group = lax.axis_index("mp")
    owner = lax.axis_index("dp")
    blocks = gradients.shape[2]
    slots = left_stats.shape[1]
    core = owner % CORES
    y = (owner // CORES) % RING
    z = owner // (CORES * RING)
    counts_row = lax.dynamic_index_in_dim(owner_counts, group, 0, keepdims=False)
    offsets_row = lax.dynamic_index_in_dim(block_offsets, group, 0, keepdims=False)
    owners_row = lax.dynamic_index_in_dim(owner_list, group, 0, keepdims=False)
    slot_ids = jnp.arange(slots, dtype=jnp.int32)
    wanted = jnp.minimum(offsets_row[:, None] + slot_ids[None, :], blocks - 1)

    summed = reduce_scatter(gradients[0, 0], z, y, core)
    received = lax.all_to_all(summed[wanted], "dp", split_axis=0, concat_axis=0, tiled=True)
    own_count = lax.dynamic_slice(counts_row, (owner,), (1,))
    new_left, new_right, updates = slot_step(own_count, received, left_stats[0], right_stats[0])
    returned = lax.all_to_all(updates, "dp", split_axis=0, concat_axis=0, tiled=True)
    returned = returned.reshape(-1, *returned.shape[2:])
    slot_of_block = jnp.arange(blocks, dtype=jnp.int32) - offsets_row[owners_row]
    placed = returned[owners_row * slots + slot_of_block]
    return new_left[None], new_right[None], gather_groups(placed, group)


def solution(mesh):
    placed = (
        P("dp", "mp", None, None, None),
        P("mp", "dp", None, None),
        P("mp", "dp", None, None),
        P(),
        P(),
        P(),
    )
    return jax.shard_map(
        per_device,
        mesh=mesh,
        in_specs=placed,
        out_specs=(P("mp", "dp", None, None), P("mp", "dp", None, None), P(None, None, "dp", None)),
        check_vma=False,
    )
```

```python
import functools

import jax
import jax.numpy as jnp
import numpy as np
from jax import lax
from jax.experimental import pallas as pl
from jax.experimental.pallas import tpu as pltpu
from jax.sharding import PartitionSpec as P

RING = 4
CORES = 2
START = 25.0 / 16.0
VMEM = 47 * 1024 * 1024
SETS = (10, 4)


def tail_coefficients():
    m1 = np.polynomial.Polynomial([1.25, -0.25])
    m2 = 1.25 - 0.25 * np.polynomial.Polynomial([0.0, 1.0]) * m1**4
    return [float(v) for v in (m1 * m2).coef]


TAIL = tail_coefficients()
EYE_PART = 1.25 * TAIL[0]


def dot(first, second, dims=((1,), (0,))):
    return lax.dot_general(
        first.astype(jnp.bfloat16),
        second.astype(jnp.bfloat16),
        (dims, ((), ())),
        preferred_element_type=jnp.float32,
    )


def roots(statistics):
    both = range(len(statistics))
    scales = [jnp.max(jnp.sum(jnp.abs(a), axis=0, keepdims=True), axis=1, keepdims=True) + 1e-06 for a in statistics]
    z = [statistics[i] * (1.0 / scales[i]) for i in both]
    zb = [z[i].astype(jnp.bfloat16) for i in both]
    square = [dot(zb[i], zb[i]) for i in both]
    e = [(0.0625 * square[i] - 0.625 * z[i]).astype(jnp.bfloat16) for i in both]
    t = [START * z[i] + dot(e[i], zb[i]) for i in both]
    y = [START * t[i] + dot(e[i], t[i]) for i in both]
    yb = [y[i].astype(jnp.bfloat16) for i in both]
    y2 = [dot(yb[i], yb[i]) for i in both]
    y3 = [dot(y2[i], yb[i]) for i in both]
    y3b = [y3[i].astype(jnp.bfloat16) for i in both]
    high = [(TAIL[6] * y3[i] + TAIL[5] * y2[i] + TAIL[4] * y[i]).astype(jnp.bfloat16) for i in both]
    q = [TAIL[1] * y[i] + TAIL[2] * y2[i] + TAIL[3] * y3[i] + dot(high[i], y3b[i]) for i in both]
    f = [1.25 * q[i] - (0.25 * TAIL[0]) * z[i] - 0.25 * dot(zb[i], q[i]) for i in both]
    return f, [1.0 / jnp.sqrt(jnp.sqrt(s)) for s in scales]


def slot_kernel(count_ref, block_ref, left_ref, right_ref, new_left_ref, new_right_ref, update_ref):
    alive = pl.program_id(0) < count_ref[0]
    extent = left_ref.shape[-1]

    @pl.when(jnp.logical_not(alive))
    def _():
        new_left_ref[...] = left_ref[...]
        new_right_ref[...] = right_ref[...]
        update_ref[...] = jnp.zeros_like(update_ref)

    @pl.when(alive)
    def _():
        block = block_ref[:, 0].reshape(extent, extent)
        fresh_left = 0.9 * left_ref[0] + (0.1 / extent) * dot(block, block, ((1,), (1,)))
        fresh_right = 0.9 * right_ref[0] + (0.1 / extent) * dot(block, block, ((0,), (0,)))
        new_left_ref[0] = fresh_left
        new_right_ref[0] = fresh_right
        (f_left, f_right), (c_left, c_right) = roots([fresh_left, fresh_right])
        half = EYE_PART * block.astype(jnp.float32) + dot(block, f_right)
        result = (EYE_PART * half + dot(f_left, half)) * (c_left * c_right)
        update_ref[:, 0] = result.astype(jnp.bfloat16).reshape(update_ref.shape[0], update_ref.shape[2], extent)


def slot_step(count, received, left, right):
    owners, slots, rows, extent = received.shape
    spread = pl.BlockSpec((owners, 1, rows, extent), lambda s, count: (0, s, 0, 0))
    whole = pl.BlockSpec((1, extent, extent), lambda s, count: (s, 0, 0))
    return pl.pallas_call(
        slot_kernel,
        grid_spec=pltpu.PrefetchScalarGridSpec(
            num_scalar_prefetch=1,
            grid=(slots,),
            in_specs=[spread, whole, whole],
            out_specs=[whole, whole, spread],
        ),
        out_shape=[
            jax.ShapeDtypeStruct(left.shape, jnp.float32),
            jax.ShapeDtypeStruct(right.shape, jnp.float32),
            jax.ShapeDtypeStruct(received.shape, jnp.bfloat16),
        ],
        compiler_params=pltpu.CompilerParams(vmem_limit_bytes=VMEM),
        cost_estimate=pl.CostEstimate(
            flops=slots * 18 * 2 * extent**3,
            bytes_accessed=4 * left.size * 4 + 2 * received.size * 2,
            transcendentals=0,
        ),
    )(count, received, left, right)


def flat(z, y, core):
    return (z * RING + y) * CORES + core


def places():
    return [(z, y, core) for z in range(RING) for y in range(RING) for core in range(CORES)]


def partner(place, core, step):
    flipped = place + 1 - 2 * (place % 2)
    mirrored = RING - 1 - place
    late = core + step - 2 * core * step
    return flipped + late * (mirrored - flipped)


def chunk(place, core, which):
    return {
        0: place,
        1: partner(place, core, 0),
        2: partner(place, core, 1),
        3: (place + RING // 2) % RING,
    }[which]


def exchange(value, axis, step):
    pairs = []
    for z, y, core in places():
        to = (partner(z, core, step), y, core) if axis == 0 else (z, partner(y, core, step), core)
        pairs.append((flat(z, y, core), flat(*to)))
    return lax.ppermute(value, "dp", pairs)


def swap(value):
    return lax.ppermute(value, "dp", [(flat(z, y, core), flat(z, y, 1 - core)) for z, y, core in places()])


def cut_specs(shape, which, half, other=False):
    _, _, _, _, rows, extent = shape
    size = SETS[half]
    start = 2 * sum(SETS[:half]) // size

    def whose(pos):
        return 1 - pos[2] if other else pos[2]

    def first(i, pos):
        return (start, 0, chunk(pos[1], whose(pos), which), whose(pos), 0, 0)

    def second(i, pos):
        return (start + 1, chunk(pos[0], whose(pos), which), 0, whose(pos), 0, 0)

    return [
        pl.BlockSpec((size, RING, 1, 1, rows, extent), first),
        pl.BlockSpec((size, 1, RING, 1, rows, extent), second),
    ]


def local_call(body, pos, in_specs, args, out_specs, out_shape, scratch=()):
    moved = sum(4 * v.size for v in out_shape)
    return pl.pallas_call(
        body,
        grid_spec=pltpu.PrefetchScalarGridSpec(
            num_scalar_prefetch=1,
            grid=(1,),
            in_specs=in_specs,
            out_specs=out_specs,
            scratch_shapes=list(scratch),
        ),
        out_shape=out_shape,
        compiler_params=pltpu.CompilerParams(vmem_limit_bytes=VMEM),
        cost_estimate=pl.CostEstimate(flops=moved, bytes_accessed=2 * moved, transcendentals=0),
    )(pos, *args)


def cut_kernel(count, pos, *refs):
    ins, outs = refs[: 2 * count], refs[2 * count :]
    for k in range(count):
        for part in (0, 1):
            outs[part][k] = ins[2 * k + part][...].reshape(outs[part].shape[1:])


def cut(view, pos, which, half):
    rows, extent = view.shape[-2:]
    shape = (len(which), SETS[half], RING, rows, extent)
    specs = [spec for w in which for spec in cut_specs(view.shape, w, half, other=True)]
    return local_call(
        functools.partial(cut_kernel, len(which)),
        pos,
        specs,
        [view] * len(specs),
        [pl.BlockSpec(shape, lambda i, pos: (0, 0, 0, 0, 0))] * 2,
        [jax.ShapeDtypeStruct(shape, jnp.bfloat16)] * 2,
    )


def add_up(own_ref, part, others):
    value = (own_ref[:, :, 0, 0] if part == 0 else own_ref[:, 0, :, 0]).astype(jnp.float32)
    for other in others:
        value = value + other.astype(jnp.float32)
    return value


def first_kernel(pos, *refs):
    views, others, outs = refs[:4], refs[4:6], refs[6:]
    for part in (0, 1):
        for k in (0, 1):
            outs[part][k] = add_up(views[2 * k + part], part, [others[part][k]]).astype(jnp.bfloat16)


def first_sums(view, pos, half, others):
    whole = pl.BlockSpec(others[0].shape, lambda i, pos: (0, 0, 0, 0, 0))
    specs = [spec for w in (3, 1) for spec in cut_specs(view.shape, w, half)]
    shape = [jax.ShapeDtypeStruct(others[0].shape, jnp.bfloat16)] * 2
    return local_call(first_kernel, pos, specs + [whole] * 2, [view] * 4 + list(others), [whole] * 2, shape)


def second_kernel(pos, *refs):
    views, others, arrived, outs = refs[:2], refs[2:4], refs[4:6], refs[6:]
    for part in (0, 1):
        outs[part][...] = add_up(views[part], part, [others[part][0], arrived[part][0]]).astype(jnp.bfloat16)


def second_sums(view, pos, half, others, arrived):
    shape = others[0].shape[1:]
    lead = pl.BlockSpec((1, *shape), lambda i, pos: (0, 0, 0, 0, 0))
    whole = pl.BlockSpec(shape, lambda i, pos: (0, 0, 0, 0))
    specs = cut_specs(view.shape, 2, half) + [lead] * 4
    out = [jax.ShapeDtypeStruct(shape, jnp.bfloat16)] * 2
    return local_call(second_kernel, pos, specs, [view] * 2 + list(others) + list(arrived), [whole] * 2, out)


def last_kernel(pos, *refs):
    views, others, direct, joined = refs[:2], refs[2:4], refs[4:6], refs[6:8]
    filled, outs, scratch = refs[8:-7], refs[-7:-1], refs[-1]
    size = scratch.shape[0]
    start = outs[1].shape[0] - size
    for earlier, out_ref in zip(filled, outs):
        if len(earlier.shape) == 4:
            out_ref[:, pl.ds(0, start)] = earlier[...]
        else:
            out_ref[pl.ds(0, start)] = earlier[...]
    for part in (0, 1):
        ahead_ref, later_ref, own_ref = outs[3 * part : 3 * part + 3]
        scratch[...] = add_up(views[part], part, [others[part][0], direct[part][0], joined[part][...]])
        place, core = pos[part], pos[2]
        here = pl.ds(start, size)
        for k, which in enumerate((3, 1)):
            ahead_ref[k, here] = scratch[:, chunk(place, core, which)].astype(jnp.bfloat16)
        later_ref[here] = scratch[:, chunk(place, core, 2)]
        own_ref[here] = scratch[:, place]


def last_sums(view, pos, half, others, direct, joined, filled):
    rows, extent = view.shape[-2:]
    shape = (SETS[half], RING, rows, extent)
    so_far = sum(SETS[: half + 1])
    tail = pl.BlockSpec((1, *shape), lambda i, pos: (1, 0, 0, 0, 0))
    whole = pl.BlockSpec(shape, lambda i, pos: (0, 0, 0, 0))

    def pieces(count):
        ahead = pl.BlockSpec((2, count, rows, extent), lambda i, pos: (0, 0, 0, 0))
        piece = pl.BlockSpec((count, rows, extent), lambda i, pos: (0, 0, 0))
        return [ahead, piece, piece] * 2

    return local_call(
        last_kernel,
        pos,
        cut_specs(view.shape, 0, half) + [tail, tail, tail, tail, whole, whole] + pieces(sum(SETS[:half]))[: len(filled)],
        [view] * 2 + [*others, *direct, *joined, *filled],
        pieces(so_far),
        [
            jax.ShapeDtypeStruct((2, so_far, rows, extent), jnp.bfloat16),
            jax.ShapeDtypeStruct((so_far, rows, extent), jnp.float32),
            jax.ShapeDtypeStruct((so_far, rows, extent), jnp.float32),
        ]
        * 2,
        [pltpu.VMEM(shape, jnp.float32)],
    )


def reduce_scatter(gradient, pos):
    blocks, extent = gradient.shape[0], gradient.shape[1]
    rows = extent // (RING * RING * CORES)
    parts = (0, 1)
    halves = range(len(SETS))
    view = gradient.reshape(blocks, RING, RING, CORES, rows, extent)
    left, swapped = view, []

    def send_across(left, which, half):
        pieces = cut(left, pos, which, half)
        left, *pieces = lax.optimization_barrier((left, *pieces))
        return left, [swap(v) for v in pieces]

    for which, half in (((3, 1), 0), ((3, 1), 1), ((2, 0), 0)):
        left, values = send_across(left, which, half)
        swapped.append(values)
    direct = []
    for half in halves:
        sums = first_sums(left, pos, half, swapped[half])
        left, *sums = lax.optimization_barrier((left, *sums))
        direct.append([exchange(v, 1 - part, 0) for part, v in zip(parts, sums)])
    left, values = send_across(left, (2, 0), 1)
    late = [swapped[2], values]
    joined, terms, pieces = [], [], []
    for half in halves:
        sums = second_sums(left, pos, half, late[half], direct[half])
        joined.append([exchange(v, 1 - part, 1) for part, v in zip(parts, sums)])
    for half in halves:
        pieces = last_sums(left, pos, half, late[half], direct[half], joined[half], pieces)
        left, *pieces = lax.optimization_barrier((left, *pieces))
    for part in parts:
        ahead, later, own = pieces[3 * part : 3 * part + 3]
        arrived = exchange(ahead, part, 0)
        more = exchange((later + arrived[0].astype(jnp.float32)).astype(jnp.bfloat16), part, 1)
        terms += [own, arrived, more]
    return terms


def place_kernel(wanted, *refs):
    *terms, out_ref, summed = refs
    for part, (own, arrived, more) in enumerate(zip(terms[::3], terms[1::3], terms[2::3])):
        value = own[...] + arrived[0].astype(jnp.float32) + more[...].astype(jnp.float32)
        value = value.astype(jnp.bfloat16)
        for half, size in enumerate(SETS):
            start = sum(SETS[:half])
            summed[pl.ds(2 * start + part * size, size)] = value[start : start + size]

    def copy(i, carry):
        out_ref[i] = summed[wanted[i]]
        return carry

    lax.fori_loop(0, out_ref.shape[0], copy, 0)


def to_slots(terms, wanted):
    rows, extent = terms[0].shape[1:]
    shape = (wanted.shape[0], rows, extent)
    specs = []
    for own in terms[::3]:
        piece = pl.BlockSpec(own.shape, lambda i, wanted: (0, 0, 0))
        lead = pl.BlockSpec((1, *own.shape), lambda i, wanted: (1, 0, 0, 0))
        specs += [piece, lead, piece]
    (out,) = local_call(
        place_kernel,
        wanted,
        specs,
        terms,
        [pl.BlockSpec(shape, lambda i, wanted: (0, 0, 0))],
        [jax.ShapeDtypeStruct(shape, jnp.bfloat16)],
        [pltpu.VMEM((2 * sum(SETS), rows, extent), jnp.bfloat16)],
    )
    return out


def send_group(value, steps):
    groups = lax.axis_size("mp")
    pairs = []
    for z, y, core in places():
        for group in range(groups):
            ahead = -steps if core else steps
            pairs.append((flat(z, y, core) * groups + group, flat(z, y, core) * groups + (group + ahead) % groups))
    return lax.ppermute(value, ("dp", "mp"), pairs)


def gather_groups(mine, group, core):
    groups = lax.axis_size("mp")
    sign = 1 - 2 * core
    mid = mine.shape[0] // 2
    behind = [send_group(mine[:mid], 1), send_group(mine[mid:], 1)]
    before = send_group(mine, -1)
    opposite = [send_group(v, 1) for v in behind]
    out = jnp.zeros((groups,) + mine.shape, mine.dtype)
    for away, values in ((0, [mine]), (-1, behind), (2, opposite), (1, [before])):
        start = 0
        for value in values:
            out = lax.dynamic_update_slice(out, value[None], ((group + sign * away + groups) % groups, start, 0, 0))
            start += mid
    return out


def per_device(gradients, left_stats, right_stats, owner_list, owner_counts, block_offsets):
    group = lax.axis_index("mp")
    owner = lax.axis_index("dp")
    blocks = gradients.shape[2]
    slots = left_stats.shape[1]
    core = owner % CORES
    y = (owner // CORES) % RING
    z = owner // (CORES * RING)
    counts_row = lax.dynamic_index_in_dim(owner_counts, group, 0, keepdims=False)
    offsets_row = lax.dynamic_index_in_dim(block_offsets, group, 0, keepdims=False)
    owners_row = lax.dynamic_index_in_dim(owner_list, group, 0, keepdims=False)
    slot_ids = jnp.arange(slots, dtype=jnp.int32)
    wanted = jnp.minimum(offsets_row[:, None] + slot_ids[None, :], blocks - 1)

    terms = reduce_scatter(gradients[0, 0], jnp.stack([z, y, core]).astype(jnp.int32))
    outgoing = to_slots(terms, wanted.reshape(-1)).reshape(-1, slots, *terms[0].shape[1:])
    received = lax.all_to_all(outgoing, "dp", split_axis=0, concat_axis=0, tiled=True)
    own_count = lax.dynamic_slice(counts_row, (owner,), (1,))
    new_left, new_right, updates = slot_step(own_count, received, left_stats[0], right_stats[0])
    returned = lax.all_to_all(updates, "dp", split_axis=0, concat_axis=0, tiled=True)
    returned = returned.reshape(-1, *returned.shape[2:])
    slot_of_block = jnp.arange(blocks, dtype=jnp.int32) - offsets_row[owners_row]
    placed = returned[owners_row * slots + slot_of_block]
    return new_left[None], new_right[None], gather_groups(placed, group, core)


def solution(mesh):
    placed = (
        P("dp", "mp", None, None, None),
        P("mp", "dp", None, None),
        P("mp", "dp", None, None),
        P(),
        P(),
        P(),
    )
    return jax.shard_map(
        per_device,
        mesh=mesh,
        in_specs=placed,
        out_specs=(P("mp", "dp", None, None), P("mp", "dp", None, None), P(None, None, "dp", None)),
        check_vma=False,
    )
```

```python
import functools

import jax
import jax.numpy as jnp
import numpy as np
from jax import lax
from jax.experimental import pallas as pl
from jax.experimental.pallas import tpu as pltpu
from jax.sharding import PartitionSpec as P

RING = 4
CORES = 2
START = 25.0 / 16.0
VMEM = 47 * 1024 * 1024
SETS = (10, 4)


def tail_coefficients():
    m1 = np.polynomial.Polynomial([1.25, -0.25])
    m2 = 1.25 - 0.25 * np.polynomial.Polynomial([0.0, 1.0]) * m1**4
    return [float(v) for v in (m1 * m2).coef]


TAIL = tail_coefficients()
EYE_PART = 1.25 * TAIL[0]


def dot(first, second, dims=((1,), (0,))):
    return lax.dot_general(
        first.astype(jnp.bfloat16),
        second.astype(jnp.bfloat16),
        (dims, ((), ())),
        preferred_element_type=jnp.float32,
    )


def mirrored(pair):
    top, low = (part.astype(jnp.bfloat16) for part in pair)
    half = low.shape[0]
    return jnp.concatenate([top, jnp.concatenate([top[:, half:].T, low], axis=1)], axis=0)


def product(first, second):
    half = first.shape[0] // 2
    return dot(first[:half], second), dot(first[half:], second[:, half:])


def mix(*terms):
    return tuple(sum(factor * pair[k] for factor, pair in terms) for k in (0, 1))


def roots(statistics):
    both = range(len(statistics))
    half = statistics[0].shape[0] // 2
    scales = [jnp.max(jnp.sum(jnp.abs(a), axis=0, keepdims=True), axis=1, keepdims=True) + 1e-06 for a in statistics]
    z = [tuple(v * (1.0 / scales[i]) for v in (statistics[i][:half], statistics[i][half:, half:])) for i in both]
    zb = [mirrored(z[i]) for i in both]
    square = [product(zb[i], zb[i]) for i in both]
    e = [mirrored(mix((0.0625, square[i]), (-0.625, z[i]))) for i in both]
    t = [mix((START, z[i]), (1.0, product(e[i], zb[i]))) for i in both]
    tb = [mirrored(t[i]) for i in both]
    y = [mix((START, t[i]), (1.0, product(e[i], tb[i]))) for i in both]
    yb = [mirrored(y[i]) for i in both]
    y2 = [product(yb[i], yb[i]) for i in both]
    y2b = [mirrored(y2[i]) for i in both]
    y3 = [product(y2b[i], yb[i]) for i in both]
    y3b = [mirrored(y3[i]) for i in both]
    high = [mirrored(mix((TAIL[6], y3[i]), (TAIL[5], y2[i]), (TAIL[4], y[i]))) for i in both]
    q = [mix((TAIL[1], y[i]), (TAIL[2], y2[i]), (TAIL[3], y3[i]), (1.0, product(high[i], y3b[i]))) for i in both]
    qb = [mirrored(q[i]) for i in both]
    f = [mirrored(mix((1.25, q[i]), (-0.25 * TAIL[0], z[i]), (-0.25, product(zb[i], qb[i])))) for i in both]
    return f, [1.0 / jnp.sqrt(jnp.sqrt(s)) for s in scales]


def slot_kernel(count_ref, block_ref, left_ref, right_ref, new_left_ref, new_right_ref, update_ref, held, sems):
    slot = pl.program_id(0)
    alive = slot < count_ref[0]
    extent = left_ref.shape[-1]
    outs = (new_left_ref, new_right_ref)

    @pl.when(jnp.logical_not(alive))
    def _():
        held[0] = left_ref[0]
        held[1] = right_ref[0]
        update_ref[...] = jnp.zeros_like(update_ref)

    @pl.when(alive)
    def _():
        block = block_ref[:, 0].reshape(extent, extent)
        low = pl.ds(extent // 2, extent // 2)
        top = pl.ds(0, extent // 2)
        rows, turned = block[: extent // 2], block[:, : extent // 2]
        held[0, top] = 0.9 * left_ref[0, top] + (0.1 / extent) * dot(rows, block, ((1,), (1,)))
        held[1, top] = 0.9 * right_ref[0, top] + (0.1 / extent) * dot(turned, block, ((0,), (0,)))
        rows, turned = block[extent // 2 :], block[:, extent // 2 :]
        held[0, low, low] = 0.9 * left_ref[0, low, low] + (0.1 / extent) * dot(rows, rows, ((1,), (1,)))
        held[1, low, low] = 0.9 * right_ref[0, low, low] + (0.1 / extent) * dot(turned, turned, ((0,), (0,)))
        held[0, low, top] = held[0, top, low].T
        held[1, low, top] = held[1, top, low].T

    stores = [pltpu.make_async_copy(held.at[k], outs[k].at[slot], sems.at[k]) for k in (0, 1)]
    for store in stores:
        store.start()

    @pl.when(alive)
    def _():
        block = block_ref[:, 0].reshape(extent, extent)
        (f_left, f_right), (c_left, c_right) = roots([held[0], held[1]])
        half = EYE_PART * block.astype(jnp.float32) + dot(block, f_right)
        result = (EYE_PART * half + dot(f_left, half)) * (c_left * c_right)
        update_ref[:, 0] = result.astype(jnp.bfloat16).reshape(update_ref.shape[0], update_ref.shape[2], extent)

    for store in stores:
        store.wait()


def slot_step(count, received, left, right):
    owners, slots, rows, extent = received.shape
    spread = pl.BlockSpec((owners, 1, rows, extent), lambda s, count: (0, s, 0, 0))
    whole = pl.BlockSpec((1, extent, extent), lambda s, count: (s, 0, 0))
    anywhere = pl.BlockSpec(memory_space=pl.ANY)
    return pl.pallas_call(
        slot_kernel,
        grid_spec=pltpu.PrefetchScalarGridSpec(
            num_scalar_prefetch=1,
            grid=(slots,),
            in_specs=[spread, whole, whole],
            out_specs=[anywhere, anywhere, spread],
            scratch_shapes=[pltpu.VMEM((2, extent, extent), jnp.float32), pltpu.SemaphoreType.DMA((2,))],
        ),
        out_shape=[
            jax.ShapeDtypeStruct(left.shape, jnp.float32),
            jax.ShapeDtypeStruct(right.shape, jnp.float32),
            jax.ShapeDtypeStruct(received.shape, jnp.bfloat16),
        ],
        compiler_params=pltpu.CompilerParams(vmem_limit_bytes=47 * 1024 * 1024),
        cost_estimate=pl.CostEstimate(
            flops=slots * 18 * 2 * extent**3,
            bytes_accessed=4 * left.size * 4 + 2 * received.size * 2,
            transcendentals=0,
        ),
    )(count, received, left, right)


def flat(z, y, core):
    return (z * RING + y) * CORES + core


def places():
    return [(z, y, core) for z in range(RING) for y in range(RING) for core in range(CORES)]


def partner(place, core, step):
    flipped = place + 1 - 2 * (place % 2)
    mirrored = RING - 1 - place
    late = core + step - 2 * core * step
    return flipped + late * (mirrored - flipped)


def chunk(place, core, which):
    return {
        0: place,
        1: partner(place, core, 0),
        2: partner(place, core, 1),
        3: (place + RING // 2) % RING,
    }[which]


def exchange(value, axis, step):
    pairs = []
    for z, y, core in places():
        to = (partner(z, core, step), y, core) if axis == 0 else (z, partner(y, core, step), core)
        pairs.append((flat(z, y, core), flat(*to)))
    return lax.ppermute(value, "dp", pairs)


def swap(value):
    return lax.ppermute(value, "dp", [(flat(z, y, core), flat(z, y, 1 - core)) for z, y, core in places()])


def cut_specs(shape, which, half, other=False):
    _, _, _, _, rows, extent = shape
    size = SETS[half]
    start = 2 * sum(SETS[:half]) // size

    def whose(pos):
        return 1 - pos[2] if other else pos[2]

    def first(i, pos):
        return (start, 0, chunk(pos[1], whose(pos), which), whose(pos), 0, 0)

    def second(i, pos):
        return (start + 1, chunk(pos[0], whose(pos), which), 0, whose(pos), 0, 0)

    return [
        pl.BlockSpec((size, RING, 1, 1, rows, extent), first),
        pl.BlockSpec((size, 1, RING, 1, rows, extent), second),
    ]


def local_call(body, pos, in_specs, args, out_specs, out_shape, scratch=()):
    moved = sum(4 * v.size for v in out_shape)
    return pl.pallas_call(
        body,
        grid_spec=pltpu.PrefetchScalarGridSpec(
            num_scalar_prefetch=1,
            grid=(1,),
            in_specs=in_specs,
            out_specs=out_specs,
            scratch_shapes=list(scratch),
        ),
        out_shape=out_shape,
        compiler_params=pltpu.CompilerParams(vmem_limit_bytes=VMEM),
        cost_estimate=pl.CostEstimate(flops=moved, bytes_accessed=2 * moved, transcendentals=0),
    )(pos, *args)


def cut_kernel(count, pos, *refs):
    ins, outs = refs[: 2 * count], refs[2 * count :]
    for k in range(count):
        for part in (0, 1):
            outs[part][k] = ins[2 * k + part][...].reshape(outs[part].shape[1:])


def cut(view, pos, which, half):
    rows, extent = view.shape[-2:]
    shape = (len(which), SETS[half], RING, rows, extent)
    specs = [spec for w in which for spec in cut_specs(view.shape, w, half, other=True)]
    return local_call(
        functools.partial(cut_kernel, len(which)),
        pos,
        specs,
        [view] * len(specs),
        [pl.BlockSpec(shape, lambda i, pos: (0, 0, 0, 0, 0))] * 2,
        [jax.ShapeDtypeStruct(shape, jnp.bfloat16)] * 2,
    )


def add_up(own_ref, part, others):
    value = (own_ref[:, :, 0, 0] if part == 0 else own_ref[:, 0, :, 0]).astype(jnp.float32)
    for other in others:
        value = value + other.astype(jnp.float32)
    return value


def first_kernel(pos, *refs):
    views, others, outs = refs[:4], refs[4:6], refs[6:]
    for part in (0, 1):
        for k in (0, 1):
            outs[part][k] = add_up(views[2 * k + part], part, [others[part][k]]).astype(jnp.bfloat16)


def first_sums(view, pos, half, others):
    whole = pl.BlockSpec(others[0].shape, lambda i, pos: (0, 0, 0, 0, 0))
    specs = [spec for w in (3, 1) for spec in cut_specs(view.shape, w, half)]
    shape = [jax.ShapeDtypeStruct(others[0].shape, jnp.bfloat16)] * 2
    return local_call(first_kernel, pos, specs + [whole] * 2, [view] * 4 + list(others), [whole] * 2, shape)


def second_kernel(pos, *refs):
    views, others, arrived, outs = refs[:2], refs[2:4], refs[4:6], refs[6:]
    for part in (0, 1):
        outs[part][...] = add_up(views[part], part, [others[part][0], arrived[part][0]]).astype(jnp.bfloat16)


def second_sums(view, pos, half, others, arrived):
    shape = others[0].shape[1:]
    lead = pl.BlockSpec((1, *shape), lambda i, pos: (0, 0, 0, 0, 0))
    whole = pl.BlockSpec(shape, lambda i, pos: (0, 0, 0, 0))
    specs = cut_specs(view.shape, 2, half) + [lead] * 4
    out = [jax.ShapeDtypeStruct(shape, jnp.bfloat16)] * 2
    return local_call(second_kernel, pos, specs, [view] * 2 + list(others) + list(arrived), [whole] * 2, out)


def rest_kernel(pos, *refs):
    views, others, direct, outs = refs[:2], refs[2:4], refs[4:6], refs[6:]
    for part in (0, 1):
        outs[part][...] = add_up(views[part], part, [others[part][0], direct[part][0]])


def rest_sums(view, pos, half, others, direct):
    shape = (SETS[half], RING, *view.shape[-2:])
    tail = pl.BlockSpec((1, *shape), lambda i, pos: (1, 0, 0, 0, 0))
    whole = pl.BlockSpec(shape, lambda i, pos: (0, 0, 0, 0))
    out = [jax.ShapeDtypeStruct(shape, jnp.float32)] * 2
    specs = cut_specs(view.shape, 0, half) + [tail] * 4
    return local_call(rest_kernel, pos, specs, [view] * 2 + [*others, *direct], [whole] * 2, out)


def last_kernel(pos, *refs):
    rest, joined = refs[:2], refs[2:4]
    filled, outs, scratch = refs[4:-7], refs[-7:-1], refs[-1]
    size = scratch.shape[0]
    start = outs[1].shape[0] - size
    for earlier, out_ref in zip(filled, outs):
        if len(earlier.shape) == 4:
            out_ref[:, pl.ds(0, start)] = earlier[...]
        else:
            out_ref[pl.ds(0, start)] = earlier[...]
    for part in (0, 1):
        ahead_ref, later_ref, own_ref = outs[3 * part : 3 * part + 3]
        scratch[...] = rest[part][...] + joined[part][...].astype(jnp.float32)
        place, core = pos[part], pos[2]
        here = pl.ds(start, size)
        for k, which in enumerate((3, 1)):
            ahead_ref[k, here] = scratch[:, chunk(place, core, which)].astype(jnp.bfloat16)
        later_ref[here] = scratch[:, chunk(place, core, 2)]
        own_ref[here] = scratch[:, place]


def last_sums(view, pos, half, rest, joined, filled):
    rows, extent = view.shape[-2:]
    shape = (SETS[half], RING, rows, extent)
    so_far = sum(SETS[: half + 1])
    whole = pl.BlockSpec(shape, lambda i, pos: (0, 0, 0, 0))

    def pieces(count):
        ahead = pl.BlockSpec((2, count, rows, extent), lambda i, pos: (0, 0, 0, 0))
        piece = pl.BlockSpec((count, rows, extent), lambda i, pos: (0, 0, 0))
        return [ahead, piece, piece] * 2

    return local_call(
        last_kernel,
        pos,
        [whole] * 4 + pieces(sum(SETS[:half]))[: len(filled)],
        [*rest, *joined, *filled],
        pieces(so_far),
        [
            jax.ShapeDtypeStruct((2, so_far, rows, extent), jnp.bfloat16),
            jax.ShapeDtypeStruct((so_far, rows, extent), jnp.float32),
            jax.ShapeDtypeStruct((so_far, rows, extent), jnp.float32),
        ]
        * 2,
        [pltpu.VMEM(shape, jnp.float32)],
    )


def reduce_scatter(gradient, pos):
    blocks, extent = gradient.shape[0], gradient.shape[1]
    rows = extent // (RING * RING * CORES)
    parts = (0, 1)
    halves = range(len(SETS))
    view = gradient.reshape(blocks, RING, RING, CORES, rows, extent)
    left, swapped = view, []

    def send_across(left, which, half):
        pieces = cut(left, pos, which, half)
        left, *pieces = lax.optimization_barrier((left, *pieces))
        return left, [swap(v) for v in pieces]

    for which, half in (((3, 1), 0), ((3, 1), 1), ((2, 0), 0)):
        left, values = send_across(left, which, half)
        swapped.append(values)
    direct = []
    for half in halves:
        sums = first_sums(left, pos, half, swapped[half])
        left, *sums = lax.optimization_barrier((left, *sums))
        direct.append([exchange(v, 1 - part, 0) for part, v in zip(parts, sums)])
    left, values = send_across(left, (2, 0), 1)
    late = [swapped[2], values]
    joined, terms, pieces = [], [], []
    for half in halves:
        sums = second_sums(left, pos, half, late[half], direct[half])
        if half + 1 < len(SETS):
            count = len(sums)
            both = lax.optimization_barrier((*sums, *direct[half + 1]))
            sums, direct[half + 1] = both[:count], both[count:]
        joined.append([exchange(v, 1 - part, 1) for part, v in zip(parts, sums)])
    rest = [rest_sums(left, pos, half, late[half], direct[half]) for half in halves]
    for half in halves:
        pieces = last_sums(left, pos, half, rest[half], joined[half], pieces)
    for part in parts:
        ahead, later, own = pieces[3 * part : 3 * part + 3]
        arrived = exchange(ahead, part, 0)
        more = exchange((later + arrived[0].astype(jnp.float32)).astype(jnp.bfloat16), part, 1)
        terms += [own, arrived, more]
    return terms


def place_kernel(wanted, *refs):
    *terms, out_ref, summed = refs
    for part, (own, arrived, more) in enumerate(zip(terms[::3], terms[1::3], terms[2::3])):
        value = own[...] + arrived[0].astype(jnp.float32) + more[...].astype(jnp.float32)
        value = value.astype(jnp.bfloat16)
        for half, size in enumerate(SETS):
            start = sum(SETS[:half])
            summed[pl.ds(2 * start + part * size, size)] = value[start : start + size]

    def copy(i, carry):
        out_ref[i] = summed[wanted[i]]
        return carry

    lax.fori_loop(0, out_ref.shape[0], copy, 0)


def to_slots(terms, wanted):
    rows, extent = terms[0].shape[1:]
    shape = (wanted.shape[0], rows, extent)
    specs = []
    for own in terms[::3]:
        piece = pl.BlockSpec(own.shape, lambda i, wanted: (0, 0, 0))
        lead = pl.BlockSpec((1, *own.shape), lambda i, wanted: (1, 0, 0, 0))
        specs += [piece, lead, piece]
    (out,) = local_call(
        place_kernel,
        wanted,
        specs,
        terms,
        [pl.BlockSpec(shape, lambda i, wanted: (0, 0, 0))],
        [jax.ShapeDtypeStruct(shape, jnp.bfloat16)],
        [pltpu.VMEM((2 * sum(SETS), rows, extent), jnp.bfloat16)],
    )
    return out


def send_group(value, steps):
    groups = lax.axis_size("mp")
    pairs = []
    for z, y, core in places():
        for group in range(groups):
            ahead = -steps if core else steps
            pairs.append((flat(z, y, core) * groups + group, flat(z, y, core) * groups + (group + ahead) % groups))
    return lax.ppermute(value, ("dp", "mp"), pairs)


def gather_groups(mine, group, core):
    groups = lax.axis_size("mp")
    sign = 1 - 2 * core
    mid = mine.shape[0] // 2
    behind = [send_group(mine[:mid], 1), send_group(mine[mid:], 1)]
    before = send_group(mine, -1)
    opposite = [send_group(v, 1) for v in behind]
    out = jnp.zeros((groups,) + mine.shape, mine.dtype)
    for away, values in ((0, [mine]), (-1, behind), (2, opposite), (1, [before])):
        start = 0
        for value in values:
            out = lax.dynamic_update_slice(out, value[None], ((group + sign * away + groups) % groups, start, 0, 0))
            start += mid
    return out


def per_device(gradients, left_stats, right_stats, owner_list, owner_counts, block_offsets):
    group = lax.axis_index("mp")
    owner = lax.axis_index("dp")
    blocks = gradients.shape[2]
    slots = left_stats.shape[1]
    core = owner % CORES
    y = (owner // CORES) % RING
    z = owner // (CORES * RING)
    counts_row = lax.dynamic_index_in_dim(owner_counts, group, 0, keepdims=False)
    offsets_row = lax.dynamic_index_in_dim(block_offsets, group, 0, keepdims=False)
    owners_row = lax.dynamic_index_in_dim(owner_list, group, 0, keepdims=False)
    slot_ids = jnp.arange(slots, dtype=jnp.int32)
    wanted = jnp.minimum(offsets_row[:, None] + slot_ids[None, :], blocks - 1)

    terms = reduce_scatter(gradients[0, 0], jnp.stack([z, y, core]).astype(jnp.int32))
    outgoing = to_slots(terms, wanted.reshape(-1)).reshape(-1, slots, *terms[0].shape[1:])
    received = lax.all_to_all(outgoing, "dp", split_axis=0, concat_axis=0, tiled=True)
    own_count = lax.dynamic_slice(counts_row, (owner,), (1,))
    new_left, new_right, updates = slot_step(own_count, received, left_stats[0], right_stats[0])
    returned = lax.all_to_all(updates, "dp", split_axis=0, concat_axis=0, tiled=True)
    returned = returned.reshape(-1, *returned.shape[2:])
    slot_of_block = jnp.arange(blocks, dtype=jnp.int32) - offsets_row[owners_row]
    placed = returned[owners_row * slots + slot_of_block]
    return new_left[None], new_right[None], gather_groups(placed, group, core)


def solution(mesh):
    placed = (
        P("dp", "mp", None, None, None),
        P("mp", "dp", None, None),
        P("mp", "dp", None, None),
        P(),
        P(),
        P(),
    )
    return jax.shard_map(
        per_device,
        mesh=mesh,
        in_specs=placed,
        out_specs=(P("mp", "dp", None, None), P("mp", "dp", None, None), P(None, None, "dp", None)),
        check_vma=False,
    )
```

```python
import functools

import jax
import jax.numpy as jnp
import numpy as np
from jax import lax
from jax.experimental import pallas as pl
from jax.experimental.pallas import tpu as pltpu
from jax.sharding import PartitionSpec as P

RING = 4
CORES = 2
START = 25.0 / 16.0
VMEM = 47 * 1024 * 1024
SETS = (10, 4)


def tail_coefficients():
    m1 = np.polynomial.Polynomial([1.25, -0.25])
    m2 = 1.25 - 0.25 * np.polynomial.Polynomial([0.0, 1.0]) * m1**4
    return [float(v) for v in (m1 * m2).coef]


TAIL = tail_coefficients()
EYE_PART = 1.25 * TAIL[0]


def dot(first, second, dims=((1,), (0,))):
    return lax.dot_general(
        first.astype(jnp.bfloat16),
        second.astype(jnp.bfloat16),
        (dims, ((), ())),
        preferred_element_type=jnp.float32,
    )


def mirrored(pair):
    top, low = (part.astype(jnp.bfloat16) for part in pair)
    half = low.shape[0]
    return jnp.concatenate([top, jnp.concatenate([top[:, half:].T, low], axis=1)], axis=0)


def product(first, second):
    half = first.shape[0] // 2
    return dot(first[:half], second), dot(first[half:], second[:, half:])


def mix(*terms):
    return tuple(sum(factor * pair[k] for factor, pair in terms) for k in (0, 1))


def roots(statistics):
    both = range(len(statistics))
    half = statistics[0].shape[0] // 2
    scales = [jnp.max(jnp.sum(jnp.abs(a), axis=0, keepdims=True), axis=1, keepdims=True) + 1e-06 for a in statistics]
    z = [tuple(v * (1.0 / scales[i]) for v in (statistics[i][:half], statistics[i][half:, half:])) for i in both]
    zb = [mirrored(z[i]) for i in both]
    square = [product(zb[i], zb[i]) for i in both]
    e = [mirrored(mix((0.0625, square[i]), (-0.625, z[i]))) for i in both]
    t = [mix((START, z[i]), (1.0, product(e[i], zb[i]))) for i in both]
    tb = [mirrored(t[i]) for i in both]
    y = [mix((START, t[i]), (1.0, product(e[i], tb[i]))) for i in both]
    yb = [mirrored(y[i]) for i in both]
    y2 = [product(yb[i], yb[i]) for i in both]
    y2b = [mirrored(y2[i]) for i in both]
    y3 = [product(y2b[i], yb[i]) for i in both]
    y3b = [mirrored(y3[i]) for i in both]
    high = [mirrored(mix((TAIL[6], y3[i]), (TAIL[5], y2[i]), (TAIL[4], y[i]))) for i in both]
    q = [mix((TAIL[1], y[i]), (TAIL[2], y2[i]), (TAIL[3], y3[i]), (1.0, product(high[i], y3b[i]))) for i in both]
    qb = [mirrored(q[i]) for i in both]
    f = [mirrored(mix((1.25, q[i]), (-0.25 * TAIL[0], z[i]), (-0.25, product(zb[i], qb[i])))) for i in both]
    return f, [1.0 / jnp.sqrt(jnp.sqrt(s)) for s in scales]


def slot_kernel(count_ref, block_ref, left_ref, right_ref, new_left_ref, new_right_ref, update_ref, held, sems):
    slot = pl.program_id(0)
    alive = slot < count_ref[0]
    extent = left_ref.shape[-1]
    outs = (new_left_ref, new_right_ref)

    @pl.when(jnp.logical_not(alive))
    def _():
        held[0] = left_ref[0]
        held[1] = right_ref[0]
        update_ref[...] = jnp.zeros_like(update_ref)

    @pl.when(alive)
    def _():
        block = block_ref[:, 0].reshape(extent, extent)
        low = pl.ds(extent // 2, extent // 2)
        top = pl.ds(0, extent // 2)
        rows, turned = block[: extent // 2], block[:, : extent // 2]
        held[0, top] = 0.9 * left_ref[0, top] + (0.1 / extent) * dot(rows, block, ((1,), (1,)))
        held[1, top] = 0.9 * right_ref[0, top] + (0.1 / extent) * dot(turned, block, ((0,), (0,)))
        rows, turned = block[extent // 2 :], block[:, extent // 2 :]
        held[0, low, low] = 0.9 * left_ref[0, low, low] + (0.1 / extent) * dot(rows, rows, ((1,), (1,)))
        held[1, low, low] = 0.9 * right_ref[0, low, low] + (0.1 / extent) * dot(turned, turned, ((0,), (0,)))
        held[0, low, top] = held[0, top, low].T
        held[1, low, top] = held[1, top, low].T

    stores = [pltpu.make_async_copy(held.at[k], outs[k].at[slot], sems.at[k]) for k in (0, 1)]
    for store in stores:
        store.start()

    @pl.when(alive)
    def _():
        block = block_ref[:, 0].reshape(extent, extent)
        (f_left, f_right), (c_left, c_right) = roots([held[0], held[1]])
        half = EYE_PART * block.astype(jnp.float32) + dot(block, f_right)
        result = (EYE_PART * half + dot(f_left, half)) * (c_left * c_right)
        update_ref[:, 0] = result.astype(jnp.bfloat16).reshape(update_ref.shape[0], update_ref.shape[2], extent)

    for store in stores:
        store.wait()


def slot_step(count, received, left, right):
    owners, slots, rows, extent = received.shape
    spread = pl.BlockSpec((owners, 1, rows, extent), lambda s, count: (0, s, 0, 0))
    whole = pl.BlockSpec((1, extent, extent), lambda s, count: (s, 0, 0))
    anywhere = pl.BlockSpec(memory_space=pl.ANY)
    return pl.pallas_call(
        slot_kernel,
        grid_spec=pltpu.PrefetchScalarGridSpec(
            num_scalar_prefetch=1,
            grid=(slots,),
            in_specs=[spread, whole, whole],
            out_specs=[anywhere, anywhere, spread],
            scratch_shapes=[pltpu.VMEM((2, extent, extent), jnp.float32), pltpu.SemaphoreType.DMA((2,))],
        ),
        out_shape=[
            jax.ShapeDtypeStruct(left.shape, jnp.float32),
            jax.ShapeDtypeStruct(right.shape, jnp.float32),
            jax.ShapeDtypeStruct(received.shape, jnp.bfloat16),
        ],
        compiler_params=pltpu.CompilerParams(vmem_limit_bytes=49 * 1024 * 1024),
        cost_estimate=pl.CostEstimate(
            flops=slots * 18 * 2 * extent**3,
            bytes_accessed=4 * left.size * 4 + 2 * received.size * 2,
            transcendentals=0,
        ),
    )(count, received, left, right)


def flat(z, y, core):
    return (z * RING + y) * CORES + core


def places():
    return [(z, y, core) for z in range(RING) for y in range(RING) for core in range(CORES)]


def partner(place, core, step):
    flipped = place + 1 - 2 * (place % 2)
    mirrored = RING - 1 - place
    late = core + step - 2 * core * step
    return flipped + late * (mirrored - flipped)


def chunk(place, core, which):
    return {
        0: place,
        1: partner(place, core, 0),
        2: partner(place, core, 1),
        3: (place + RING // 2) % RING,
    }[which]


def exchange(value, axis, step):
    pairs = []
    for z, y, core in places():
        to = (partner(z, core, step), y, core) if axis == 0 else (z, partner(y, core, step), core)
        pairs.append((flat(z, y, core), flat(*to)))
    return lax.ppermute(value, "dp", pairs)


def swap(value):
    return lax.ppermute(value, "dp", [(flat(z, y, core), flat(z, y, 1 - core)) for z, y, core in places()])


def cut_specs(shape, which, half, other=False):
    _, _, _, _, rows, extent = shape
    size = SETS[half]
    start = 2 * sum(SETS[:half]) // size

    def whose(pos):
        return 1 - pos[2] if other else pos[2]

    def first(i, pos):
        return (start, 0, chunk(pos[1], whose(pos), which), whose(pos), 0, 0)

    def second(i, pos):
        return (start + 1, chunk(pos[0], whose(pos), which), 0, whose(pos), 0, 0)

    return [
        pl.BlockSpec((size, RING, 1, 1, rows, extent), first),
        pl.BlockSpec((size, 1, RING, 1, rows, extent), second),
    ]


def local_call(body, pos, in_specs, args, out_specs, out_shape, scratch=()):
    moved = sum(4 * v.size for v in out_shape)
    return pl.pallas_call(
        body,
        grid_spec=pltpu.PrefetchScalarGridSpec(
            num_scalar_prefetch=1,
            grid=(1,),
            in_specs=in_specs,
            out_specs=out_specs,
            scratch_shapes=list(scratch),
        ),
        out_shape=out_shape,
        compiler_params=pltpu.CompilerParams(vmem_limit_bytes=VMEM),
        cost_estimate=pl.CostEstimate(flops=moved, bytes_accessed=2 * moved, transcendentals=0),
    )(pos, *args)


def cut_kernel(count, pos, *refs):
    ins, outs = refs[: 2 * count], refs[2 * count :]
    for k in range(count):
        for part in (0, 1):
            outs[part][k] = ins[2 * k + part][...].reshape(outs[part].shape[1:])


def cut(view, pos, which, half):
    rows, extent = view.shape[-2:]
    shape = (len(which), SETS[half], RING, rows, extent)
    specs = [spec for w in which for spec in cut_specs(view.shape, w, half, other=True)]
    return local_call(
        functools.partial(cut_kernel, len(which)),
        pos,
        specs,
        [view] * len(specs),
        [pl.BlockSpec(shape, lambda i, pos: (0, 0, 0, 0, 0))] * 2,
        [jax.ShapeDtypeStruct(shape, jnp.bfloat16)] * 2,
    )


def add_up(own_ref, part, others):
    value = (own_ref[:, :, 0, 0] if part == 0 else own_ref[:, 0, :, 0]).astype(jnp.float32)
    for other in others:
        value = value + other.astype(jnp.float32)
    return value


def first_kernel(pos, *refs):
    views, others, outs = refs[:4], refs[4:6], refs[6:]
    for part in (0, 1):
        for k in (0, 1):
            outs[part][k] = add_up(views[2 * k + part], part, [others[part][k]]).astype(jnp.bfloat16)


def first_sums(view, pos, half, others):
    whole = pl.BlockSpec(others[0].shape, lambda i, pos: (0, 0, 0, 0, 0))
    specs = [spec for w in (3, 1) for spec in cut_specs(view.shape, w, half)]
    shape = [jax.ShapeDtypeStruct(others[0].shape, jnp.bfloat16)] * 2
    return local_call(first_kernel, pos, specs + [whole] * 2, [view] * 4 + list(others), [whole] * 2, shape)


def second_kernel(pos, *refs):
    views, others, arrived, outs = refs[:2], refs[2:4], refs[4:6], refs[6:]
    for part in (0, 1):
        outs[part][...] = add_up(views[part], part, [others[part][0], arrived[part][0]]).astype(jnp.bfloat16)


def second_sums(view, pos, half, others, arrived):
    shape = others[0].shape[1:]
    lead = pl.BlockSpec((1, *shape), lambda i, pos: (0, 0, 0, 0, 0))
    whole = pl.BlockSpec(shape, lambda i, pos: (0, 0, 0, 0))
    specs = cut_specs(view.shape, 2, half) + [lead] * 4
    out = [jax.ShapeDtypeStruct(shape, jnp.bfloat16)] * 2
    return local_call(second_kernel, pos, specs, [view] * 2 + list(others) + list(arrived), [whole] * 2, out)


def rest_kernel(pos, *refs):
    views, others, direct, outs = refs[:2], refs[2:4], refs[4:6], refs[6:]
    for part in (0, 1):
        outs[part][...] = add_up(views[part], part, [others[part][0], direct[part][0]])


def rest_sums(view, pos, half, others, direct):
    shape = (SETS[half], RING, *view.shape[-2:])
    tail = pl.BlockSpec((1, *shape), lambda i, pos: (1, 0, 0, 0, 0))
    whole = pl.BlockSpec(shape, lambda i, pos: (0, 0, 0, 0))
    out = [jax.ShapeDtypeStruct(shape, jnp.float32)] * 2
    specs = cut_specs(view.shape, 0, half) + [tail] * 4
    return local_call(rest_kernel, pos, specs, [view] * 2 + [*others, *direct], [whole] * 2, out)


def last_kernel(pos, *refs):
    rest, joined = refs[:2], refs[2:4]
    filled, outs, scratch = refs[4:-7], refs[-7:-1], refs[-1]
    size = scratch.shape[0]
    start = outs[1].shape[0] - size
    for earlier, out_ref in zip(filled, outs):
        if len(earlier.shape) == 4:
            out_ref[:, pl.ds(0, start)] = earlier[...]
        else:
            out_ref[pl.ds(0, start)] = earlier[...]
    for part in (0, 1):
        ahead_ref, later_ref, own_ref = outs[3 * part : 3 * part + 3]
        scratch[...] = rest[part][...] + joined[part][...].astype(jnp.float32)
        place, core = pos[part], pos[2]
        here = pl.ds(start, size)
        for k, which in enumerate((3, 1)):
            ahead_ref[k, here] = scratch[:, chunk(place, core, which)].astype(jnp.bfloat16)
        later_ref[here] = scratch[:, chunk(place, core, 2)]
        own_ref[here] = scratch[:, place]


def last_sums(view, pos, half, rest, joined, filled):
    rows, extent = view.shape[-2:]
    shape = (SETS[half], RING, rows, extent)
    so_far = sum(SETS[: half + 1])
    whole = pl.BlockSpec(shape, lambda i, pos: (0, 0, 0, 0))

    def pieces(count):
        ahead = pl.BlockSpec((2, count, rows, extent), lambda i, pos: (0, 0, 0, 0))
        piece = pl.BlockSpec((count, rows, extent), lambda i, pos: (0, 0, 0))
        return [ahead, piece, piece] * 2

    return local_call(
        last_kernel,
        pos,
        [whole] * 4 + pieces(sum(SETS[:half]))[: len(filled)],
        [*rest, *joined, *filled],
        pieces(so_far),
        [
            jax.ShapeDtypeStruct((2, so_far, rows, extent), jnp.bfloat16),
            jax.ShapeDtypeStruct((so_far, rows, extent), jnp.float32),
            jax.ShapeDtypeStruct((so_far, rows, extent), jnp.float32),
        ]
        * 2,
        [pltpu.VMEM(shape, jnp.float32)],
    )


def reduce_scatter(gradient, pos):
    blocks, extent = gradient.shape[0], gradient.shape[1]
    rows = extent // (RING * RING * CORES)
    parts = (0, 1)
    halves = range(len(SETS))
    view = gradient.reshape(blocks, RING, RING, CORES, rows, extent)
    left, swapped = view, []

    def send_across(left, which, half):
        pieces = cut(left, pos, which, half)
        left, *pieces = lax.optimization_barrier((left, *pieces))
        return left, [swap(v) for v in pieces]

    for which, half in (((3, 1), 0), ((3, 1), 1), ((2, 0), 0)):
        left, values = send_across(left, which, half)
        swapped.append(values)
    direct = []
    for half in halves:
        sums = first_sums(left, pos, half, swapped[half])
        left, *sums = lax.optimization_barrier((left, *sums))
        direct.append([exchange(v, 1 - part, 0) for part, v in zip(parts, sums)])
    left, values = send_across(left, (2, 0), 1)
    late = [swapped[2], values]
    joined, terms, pieces = [], [], []
    for half in halves:
        sums = second_sums(left, pos, half, late[half], direct[half])
        if half + 1 < len(SETS):
            count = len(sums)
            both = lax.optimization_barrier((*sums, *direct[half + 1]))
            sums, direct[half + 1] = both[:count], both[count:]
        joined.append([exchange(v, 1 - part, 1) for part, v in zip(parts, sums)])
    rest = [rest_sums(left, pos, half, late[half], direct[half]) for half in halves]
    for half in halves:
        pieces = last_sums(left, pos, half, rest[half], joined[half], pieces)
    for part in parts:
        ahead, later, own = pieces[3 * part : 3 * part + 3]
        arrived = exchange(ahead, part, 0)
        more = exchange((later + arrived[0].astype(jnp.float32)).astype(jnp.bfloat16), part, 1)
        terms += [own, arrived, more]
    return terms


def place_kernel(wanted, *refs):
    *terms, out_ref, summed = refs
    for part, (own, arrived, more) in enumerate(zip(terms[::3], terms[1::3], terms[2::3])):
        value = own[...] + arrived[0].astype(jnp.float32) + more[...].astype(jnp.float32)
        value = value.astype(jnp.bfloat16)
        for half, size in enumerate(SETS):
            start = sum(SETS[:half])
            summed[pl.ds(2 * start + part * size, size)] = value[start : start + size]

    def copy(i, carry):
        out_ref[i] = summed[wanted[i]]
        return carry

    lax.fori_loop(0, out_ref.shape[0], copy, 0)


def to_slots(terms, wanted):
    rows, extent = terms[0].shape[1:]
    shape = (wanted.shape[0], rows, extent)
    specs = []
    for own in terms[::3]:
        piece = pl.BlockSpec(own.shape, lambda i, wanted: (0, 0, 0))
        lead = pl.BlockSpec((1, *own.shape), lambda i, wanted: (1, 0, 0, 0))
        specs += [piece, lead, piece]
    (out,) = local_call(
        place_kernel,
        wanted,
        specs,
        terms,
        [pl.BlockSpec(shape, lambda i, wanted: (0, 0, 0))],
        [jax.ShapeDtypeStruct(shape, jnp.bfloat16)],
        [pltpu.VMEM((2 * sum(SETS), rows, extent), jnp.bfloat16)],
    )
    return out


def send_group(value, steps):
    groups = lax.axis_size("mp")
    pairs = []
    for z, y, core in places():
        for group in range(groups):
            ahead = -steps if core else steps
            pairs.append((flat(z, y, core) * groups + group, flat(z, y, core) * groups + (group + ahead) % groups))
    return lax.ppermute(value, ("dp", "mp"), pairs)


def gather_groups(mine, group, core):
    groups = lax.axis_size("mp")
    sign = 1 - 2 * core
    mid = mine.shape[0] // 2
    behind = [send_group(mine[:mid], 1), send_group(mine[mid:], 1)]
    before = send_group(mine, -1)
    opposite = [send_group(v, 1) for v in behind]
    out = jnp.zeros((groups,) + mine.shape, mine.dtype)
    for away, values in ((0, [mine]), (-1, behind), (2, opposite), (1, [before])):
        start = 0
        for value in values:
            out = lax.dynamic_update_slice(out, value[None], ((group + sign * away + groups) % groups, start, 0, 0))
            start += mid
    return out


def per_device(gradients, left_stats, right_stats, owner_list, owner_counts, block_offsets):
    group = lax.axis_index("mp")
    owner = lax.axis_index("dp")
    blocks = gradients.shape[2]
    slots = left_stats.shape[1]
    core = owner % CORES
    y = (owner // CORES) % RING
    z = owner // (CORES * RING)
    counts_row = lax.dynamic_index_in_dim(owner_counts, group, 0, keepdims=False)
    offsets_row = lax.dynamic_index_in_dim(block_offsets, group, 0, keepdims=False)
    owners_row = lax.dynamic_index_in_dim(owner_list, group, 0, keepdims=False)
    slot_ids = jnp.arange(slots, dtype=jnp.int32)
    wanted = jnp.minimum(offsets_row[:, None] + slot_ids[None, :], blocks - 1)

    terms = reduce_scatter(gradients[0, 0], jnp.stack([z, y, core]).astype(jnp.int32))
    outgoing = to_slots(terms, wanted.reshape(-1)).reshape(-1, slots, *terms[0].shape[1:])
    received = lax.all_to_all(outgoing, "dp", split_axis=0, concat_axis=0, tiled=True)
    own_count = lax.dynamic_slice(counts_row, (owner,), (1,))
    new_left, new_right, updates = slot_step(own_count, received, left_stats[0], right_stats[0])
    returned = lax.all_to_all(updates, "dp", split_axis=0, concat_axis=0, tiled=True)
    returned = returned.reshape(-1, *returned.shape[2:])
    slot_of_block = jnp.arange(blocks, dtype=jnp.int32) - offsets_row[owners_row]
    placed = returned[owners_row * slots + slot_of_block]
    return new_left[None], new_right[None], gather_groups(placed, group, core)


def solution(mesh):
    placed = (
        P("dp", "mp", None, None, None),
        P("mp", "dp", None, None),
        P("mp", "dp", None, None),
        P(),
        P(),
        P(),
    )
    return jax.shard_map(
        per_device,
        mesh=mesh,
        in_specs=placed,
        out_specs=(P("mp", "dp", None, None), P("mp", "dp", None, None), P(None, None, "dp", None)),
        check_vma=False,
    )
```

```python
import functools

import jax
import jax.numpy as jnp
import numpy as np
from jax import lax
from jax.experimental import pallas as pl
from jax.experimental.pallas import tpu as pltpu
from jax.sharding import PartitionSpec as P

RING = 4
CORES = 2
START = 25.0 / 16.0
VMEM = 47 * 1024 * 1024
SETS = (10, 4)
PLACES = 2


def tail_coefficients():
    m1 = np.polynomial.Polynomial([1.25, -0.25])
    m2 = 1.25 - 0.25 * np.polynomial.Polynomial([0.0, 1.0]) * m1**4
    return [float(v) for v in (m1 * m2).coef]


TAIL = tail_coefficients()
EYE_PART = 1.25 * TAIL[0]


def dot(first, second, dims=((1,), (0,))):
    return lax.dot_general(
        first.astype(jnp.bfloat16),
        second.astype(jnp.bfloat16),
        (dims, ((), ())),
        preferred_element_type=jnp.float32,
    )


def mirrored(pair):
    top, low = (part.astype(jnp.bfloat16) for part in pair)
    half = low.shape[0]
    return jnp.concatenate([top, jnp.concatenate([top[:, half:].T, low], axis=1)], axis=0)


def product(first, second):
    half = first.shape[0] // 2
    return dot(first[:half], second), dot(first[half:], second[:, half:])


def mix(*terms):
    return tuple(sum(factor * pair[k] for factor, pair in terms) for k in (0, 1))


def roots(statistics):
    both = range(len(statistics))
    half = statistics[0].shape[0] // 2
    scales = [jnp.max(jnp.sum(jnp.abs(a), axis=0, keepdims=True), axis=1, keepdims=True) + 1e-06 for a in statistics]
    z = [tuple(v * (1.0 / scales[i]) for v in (statistics[i][:half], statistics[i][half:, half:])) for i in both]
    zb = [mirrored(z[i]) for i in both]
    square = [product(zb[i], zb[i]) for i in both]
    e = [mirrored(mix((0.0625, square[i]), (-0.625, z[i]))) for i in both]
    t = [mix((START, z[i]), (1.0, product(e[i], zb[i]))) for i in both]
    tb = [mirrored(t[i]) for i in both]
    y = [mix((START, t[i]), (1.0, product(e[i], tb[i]))) for i in both]
    yb = [mirrored(y[i]) for i in both]
    y2 = [product(yb[i], yb[i]) for i in both]
    y2b = [mirrored(y2[i]) for i in both]
    y3 = [product(y2b[i], yb[i]) for i in both]
    y3b = [mirrored(y3[i]) for i in both]
    high = [mirrored(mix((TAIL[6], y3[i]), (TAIL[5], y2[i]), (TAIL[4], y[i]))) for i in both]
    q = [mix((TAIL[1], y[i]), (TAIL[2], y2[i]), (TAIL[3], y3[i]), (1.0, product(high[i], y3b[i]))) for i in both]
    qb = [mirrored(q[i]) for i in both]
    f = [mirrored(mix((1.25, q[i]), (-0.25 * TAIL[0], z[i]), (-0.25, product(zb[i], qb[i])))) for i in both]
    return f, [1.0 / jnp.sqrt(jnp.sqrt(s)) for s in scales]


def slot_kernel(count_ref, block_ref, left_ref, right_ref, new_left_ref, new_right_ref, update_ref, held, sems):
    slot = pl.program_id(0)
    alive = slot < count_ref[0]
    extent = left_ref.shape[-1]
    outs = (new_left_ref, new_right_ref)

    @pl.when(jnp.logical_not(alive))
    def _():
        held[0] = left_ref[0]
        held[1] = right_ref[0]
        update_ref[...] = jnp.zeros_like(update_ref)

    @pl.when(alive)
    def _():
        block = block_ref[:, 0].reshape(extent, extent)
        low = pl.ds(extent // 2, extent // 2)
        top = pl.ds(0, extent // 2)
        rows, turned = block[: extent // 2], block[:, : extent // 2]
        held[0, top] = 0.9 * left_ref[0, top] + (0.1 / extent) * dot(rows, block, ((1,), (1,)))
        held[1, top] = 0.9 * right_ref[0, top] + (0.1 / extent) * dot(turned, block, ((0,), (0,)))
        rows, turned = block[extent // 2 :], block[:, extent // 2 :]
        held[0, low, low] = 0.9 * left_ref[0, low, low] + (0.1 / extent) * dot(rows, rows, ((1,), (1,)))
        held[1, low, low] = 0.9 * right_ref[0, low, low] + (0.1 / extent) * dot(turned, turned, ((0,), (0,)))
        held[0, low, top] = held[0, top, low].T
        held[1, low, top] = held[1, top, low].T

    stores = [pltpu.make_async_copy(held.at[k], outs[k].at[slot], sems.at[k]) for k in (0, 1)]
    for store in stores:
        store.start()

    @pl.when(alive)
    def _():
        block = block_ref[:, 0].reshape(extent, extent)
        (f_left, f_right), (c_left, c_right) = roots([held[0], held[1]])
        half = EYE_PART * block.astype(jnp.float32) + dot(block, f_right)
        result = (EYE_PART * half + dot(f_left, half)) * (c_left * c_right)
        update_ref[:, 0] = result.astype(jnp.bfloat16).reshape(update_ref.shape[0], update_ref.shape[2], extent)

    for store in stores:
        store.wait()


def slot_step(count, received, left, right):
    owners, slots, rows, extent = received.shape
    spread = pl.BlockSpec((owners, 1, rows, extent), lambda s, count: (0, s, 0, 0))
    whole = pl.BlockSpec((1, extent, extent), lambda s, count: (s, 0, 0))
    anywhere = pl.BlockSpec(memory_space=pl.ANY)
    return pl.pallas_call(
        slot_kernel,
        grid_spec=pltpu.PrefetchScalarGridSpec(
            num_scalar_prefetch=1,
            grid=(slots,),
            in_specs=[spread, whole, whole],
            out_specs=[anywhere, anywhere, spread],
            scratch_shapes=[pltpu.VMEM((2, extent, extent), jnp.float32), pltpu.SemaphoreType.DMA((2,))],
        ),
        out_shape=[
            jax.ShapeDtypeStruct(left.shape, jnp.float32),
            jax.ShapeDtypeStruct(right.shape, jnp.float32),
            jax.ShapeDtypeStruct(received.shape, jnp.bfloat16),
        ],
        compiler_params=pltpu.CompilerParams(vmem_limit_bytes=49 * 1024 * 1024),
        cost_estimate=pl.CostEstimate(
            flops=slots * 18 * 2 * extent**3,
            bytes_accessed=4 * left.size * 4 + 2 * received.size * 2,
            transcendentals=0,
        ),
    )(count, received, left, right)


def flat(z, y, core):
    return (z * RING + y) * CORES + core


def places():
    return [(z, y, core) for z in range(RING) for y in range(RING) for core in range(CORES)]


def partner(place, core, step):
    flipped = place + 1 - 2 * (place % 2)
    mirrored = RING - 1 - place
    late = core + step - 2 * core * step
    return flipped + late * (mirrored - flipped)


def chunk(place, core, which):
    return {
        0: place,
        1: partner(place, core, 0),
        2: partner(place, core, 1),
        3: (place + RING // 2) % RING,
    }[which]


def exchange(value, axis, step):
    pairs = []
    for z, y, core in places():
        to = (partner(z, core, step), y, core) if axis == 0 else (z, partner(y, core, step), core)
        pairs.append((flat(z, y, core), flat(*to)))
    return lax.ppermute(value, "dp", pairs)


def swap(value):
    return lax.ppermute(value, "dp", [(flat(z, y, core), flat(z, y, 1 - core)) for z, y, core in places()])


def cut_specs(shape, which, half, other=False):
    _, _, _, _, rows, extent = shape
    size = SETS[half]
    start = 2 * sum(SETS[:half]) // size

    def whose(pos):
        return 1 - pos[2] if other else pos[2]

    def first(i, pos):
        return (start, 0, chunk(pos[1], whose(pos), which), whose(pos), 0, 0)

    def second(i, pos):
        return (start + 1, chunk(pos[0], whose(pos), which), 0, whose(pos), 0, 0)

    return [
        pl.BlockSpec((size, RING, 1, 1, rows, extent), first),
        pl.BlockSpec((size, 1, RING, 1, rows, extent), second),
    ]


def local_call(body, pos, in_specs, args, out_specs, out_shape, scratch=(), steps=1):
    moved = sum(4 * v.size for v in out_shape)
    return pl.pallas_call(
        body,
        grid_spec=pltpu.PrefetchScalarGridSpec(
            num_scalar_prefetch=1,
            grid=(steps,),
            in_specs=in_specs,
            out_specs=out_specs,
            scratch_shapes=list(scratch),
        ),
        out_shape=out_shape,
        compiler_params=pltpu.CompilerParams(vmem_limit_bytes=VMEM),
        cost_estimate=pl.CostEstimate(flops=moved, bytes_accessed=2 * moved, transcendentals=0),
    )(pos, *args)


def cut_kernel(count, pos, *refs):
    ins, outs = refs[: 2 * count], refs[2 * count :]
    for k in range(count):
        for part in (0, 1):
            outs[part][k] = ins[2 * k + part][...].reshape(outs[part].shape[1:])


def cut(view, pos, which, half):
    rows, extent = view.shape[-2:]
    shape = (len(which), SETS[half], RING, rows, extent)
    specs = [spec for w in which for spec in cut_specs(view.shape, w, half, other=True)]
    return local_call(
        functools.partial(cut_kernel, len(which)),
        pos,
        specs,
        [view] * len(specs),
        [pl.BlockSpec(shape, lambda i, pos: (0, 0, 0, 0, 0))] * 2,
        [jax.ShapeDtypeStruct(shape, jnp.bfloat16)] * 2,
    )


def add_up(own_ref, part, others):
    value = (own_ref[:, :, 0, 0] if part == 0 else own_ref[:, 0, :, 0]).astype(jnp.float32)
    for other in others:
        value = value + other.astype(jnp.float32)
    return value


def first_kernel(pos, *refs):
    views, others, outs = refs[:4], refs[4:6], refs[6:]
    for part in (0, 1):
        for k in (0, 1):
            outs[part][k] = add_up(views[2 * k + part], part, [others[part][k]]).astype(jnp.bfloat16)


def first_sums(view, pos, half, others):
    whole = pl.BlockSpec(others[0].shape, lambda i, pos: (0, 0, 0, 0, 0))
    specs = [spec for w in (3, 1) for spec in cut_specs(view.shape, w, half)]
    shape = [jax.ShapeDtypeStruct(others[0].shape, jnp.bfloat16)] * 2
    return local_call(first_kernel, pos, specs + [whole] * 2, [view] * 4 + list(others), [whole] * 2, shape)


def second_kernel(pos, *refs):
    views, others, arrived, outs = refs[:2], refs[2:4], refs[4:6], refs[6:]
    for part in (0, 1):
        outs[part][...] = add_up(views[part], part, [others[part][0], arrived[part][0]]).astype(jnp.bfloat16)


def second_sums(view, pos, half, others, arrived):
    shape = others[0].shape[1:]
    lead = pl.BlockSpec((1, *shape), lambda i, pos: (0, 0, 0, 0, 0))
    whole = pl.BlockSpec(shape, lambda i, pos: (0, 0, 0, 0))
    specs = cut_specs(view.shape, 2, half) + [lead] * 4
    out = [jax.ShapeDtypeStruct(shape, jnp.bfloat16)] * 2
    return local_call(second_kernel, pos, specs, [view] * 2 + list(others) + list(arrived), [whole] * 2, out)


def rest_kernel(pos, *refs):
    views, others, direct, outs = refs[:2], refs[2:4], refs[4:6], refs[6:]
    for part in (0, 1):
        outs[part][...] = add_up(views[part], part, [others[part][0], direct[part][0]])


def rest_sums(view, pos, half, others, direct):
    shape = (SETS[half], RING, *view.shape[-2:])
    tail = pl.BlockSpec((1, *shape), lambda i, pos: (1, 0, 0, 0, 0))
    whole = pl.BlockSpec(shape, lambda i, pos: (0, 0, 0, 0))
    out = [jax.ShapeDtypeStruct(shape, jnp.float32)] * 2
    specs = cut_specs(view.shape, 0, half) + [tail] * 4
    return local_call(rest_kernel, pos, specs, [view] * 2 + [*others, *direct], [whole] * 2, out)


def last_kernel(pos, *refs):
    rest, joined = refs[:2], refs[2:4]
    filled, outs, scratch = refs[4:-7], refs[-7:-1], refs[-1]
    size = scratch.shape[0]
    start = outs[1].shape[0] - size
    for earlier, out_ref in zip(filled, outs):
        if len(earlier.shape) == 4:
            out_ref[:, pl.ds(0, start)] = earlier[...]
        else:
            out_ref[pl.ds(0, start)] = earlier[...]
    for part in (0, 1):
        ahead_ref, later_ref, own_ref = outs[3 * part : 3 * part + 3]
        scratch[...] = rest[part][...] + joined[part][...].astype(jnp.float32)
        place, core = pos[part], pos[2]
        here = pl.ds(start, size)
        for k, which in enumerate((3, 1)):
            ahead_ref[k, here] = scratch[:, chunk(place, core, which)].astype(jnp.bfloat16)
        later_ref[here] = scratch[:, chunk(place, core, 2)]
        own_ref[here] = scratch[:, place]


def last_sums(view, pos, half, rest, joined, filled):
    rows, extent = view.shape[-2:]
    shape = (SETS[half], RING, rows, extent)
    so_far = sum(SETS[: half + 1])
    whole = pl.BlockSpec(shape, lambda i, pos: (0, 0, 0, 0))

    def pieces(count):
        ahead = pl.BlockSpec((2, count, rows, extent), lambda i, pos: (0, 0, 0, 0))
        piece = pl.BlockSpec((count, rows, extent), lambda i, pos: (0, 0, 0))
        return [ahead, piece, piece] * 2

    return local_call(
        last_kernel,
        pos,
        [whole] * 4 + pieces(sum(SETS[:half]))[: len(filled)],
        [*rest, *joined, *filled],
        pieces(so_far),
        [
            jax.ShapeDtypeStruct((2, so_far, rows, extent), jnp.bfloat16),
            jax.ShapeDtypeStruct((so_far, rows, extent), jnp.float32),
            jax.ShapeDtypeStruct((so_far, rows, extent), jnp.float32),
        ]
        * 2,
        [pltpu.VMEM(shape, jnp.float32)],
    )


def reduce_scatter(gradient, pos):
    blocks, extent = gradient.shape[0], gradient.shape[1]
    rows = extent // (RING * RING * CORES)
    parts = (0, 1)
    halves = range(len(SETS))
    view = gradient.reshape(blocks, RING, RING, CORES, rows, extent)
    left, swapped = view, []

    def send_across(left, which, half):
        pieces = cut(left, pos, which, half)
        left, *pieces = lax.optimization_barrier((left, *pieces))
        return left, [swap(v) for v in pieces]

    for which, half in (((3, 1), 0), ((3, 1), 1), ((2, 0), 0)):
        left, values = send_across(left, which, half)
        swapped.append(values)
    direct = []
    for half in halves:
        sums = first_sums(left, pos, half, swapped[half])
        left, *sums = lax.optimization_barrier((left, *sums))
        direct.append([exchange(v, 1 - part, 0) for part, v in zip(parts, sums)])
    left, values = send_across(left, (2, 0), 1)
    late = [swapped[2], values]
    joined, terms, pieces = [], [], []
    for half in halves:
        sums = second_sums(left, pos, half, late[half], direct[half])
        if half + 1 < len(SETS):
            count = len(sums)
            both = lax.optimization_barrier((*sums, *direct[half + 1]))
            sums, direct[half + 1] = both[:count], both[count:]
        joined.append([exchange(v, 1 - part, 1) for part, v in zip(parts, sums)])
    rest = [rest_sums(left, pos, half, late[half], direct[half]) for half in halves]
    for half in halves:
        pieces = last_sums(left, pos, half, rest[half], joined[half], pieces)
    for part in parts:
        ahead, later, own = pieces[3 * part : 3 * part + 3]
        arrived = exchange(ahead, part, 0)
        more = exchange((later + arrived[0].astype(jnp.float32)).astype(jnp.bfloat16), part, 1)
        terms += [own, arrived, more]
    return terms


def place_kernel(wanted, *refs):
    *terms, out_ref, summed = refs
    @pl.when(pl.program_id(0) == 0)
    def _():
        for part, (own, arrived, more) in enumerate(zip(terms[::3], terms[1::3], terms[2::3])):
            value = own[...] + arrived[0].astype(jnp.float32) + more[...].astype(jnp.float32)
            value = value.astype(jnp.bfloat16)
            for half, size in enumerate(SETS):
                start = sum(SETS[:half])
                summed[pl.ds(2 * start + part * size, size)] = value[start : start + size]

    first = pl.program_id(0) * out_ref.shape[0]

    def copy(i, carry):
        out_ref[i] = summed[wanted[first + i]]
        return carry

    lax.fori_loop(0, out_ref.shape[0], copy, 0)


def to_slots(terms, wanted):
    rows, extent = terms[0].shape[1:]
    shape = (wanted.shape[0], rows, extent)
    specs = []
    for own in terms[::3]:
        piece = pl.BlockSpec(own.shape, lambda i, wanted: (0, 0, 0))
        lead = pl.BlockSpec((1, *own.shape), lambda i, wanted: (1, 0, 0, 0))
        specs += [piece, lead, piece]
    (out,) = local_call(
        place_kernel,
        wanted,
        specs,
        terms,
        [pl.BlockSpec((shape[0] // PLACES, *shape[1:]), lambda i, wanted: (i, 0, 0))],
        [jax.ShapeDtypeStruct(shape, jnp.bfloat16)],
        [pltpu.VMEM((2 * sum(SETS), rows, extent), jnp.bfloat16)],
        PLACES,
    )
    return out


def send_group(value, steps):
    groups = lax.axis_size("mp")
    pairs = []
    for z, y, core in places():
        for group in range(groups):
            ahead = -steps if core else steps
            pairs.append((flat(z, y, core) * groups + group, flat(z, y, core) * groups + (group + ahead) % groups))
    return lax.ppermute(value, ("dp", "mp"), pairs)


def gather_groups(halves, group, core):
    groups = lax.axis_size("mp")
    sign = 1 - 2 * core
    size = halves[0].shape[0]
    behind = [send_group(v, 1) for v in halves]
    before = [send_group(v, -1) for v in halves]
    opposite = [send_group(v, 1) for v in behind]
    out = jnp.zeros((groups, size * len(halves), *halves[0].shape[1:]), halves[0].dtype)
    for away, values in ((0, halves), (-1, behind), (2, opposite), (1, before)):
        for k, value in enumerate(values):
            place = ((group + sign * away + groups) % groups, size * k, 0, 0)
            out = lax.dynamic_update_slice(out, value[None], place)
    return out


def per_device(gradients, left_stats, right_stats, owner_list, owner_counts, block_offsets):
    group = lax.axis_index("mp")
    owner = lax.axis_index("dp")
    blocks = gradients.shape[2]
    slots = left_stats.shape[1]
    core = owner % CORES
    y = (owner // CORES) % RING
    z = owner // (CORES * RING)
    counts_row = lax.dynamic_index_in_dim(owner_counts, group, 0, keepdims=False)
    offsets_row = lax.dynamic_index_in_dim(block_offsets, group, 0, keepdims=False)
    owners_row = lax.dynamic_index_in_dim(owner_list, group, 0, keepdims=False)
    slot_ids = jnp.arange(slots, dtype=jnp.int32)
    wanted = jnp.minimum(offsets_row[:, None] + slot_ids[None, :], blocks - 1)

    terms = reduce_scatter(gradients[0, 0], jnp.stack([z, y, core]).astype(jnp.int32))
    outgoing = to_slots(terms, wanted.reshape(-1)).reshape(-1, slots, *terms[0].shape[1:])
    received = lax.all_to_all(outgoing, "dp", split_axis=0, concat_axis=0, tiled=True)
    own_count = lax.dynamic_slice(counts_row, (owner,), (1,))
    new_left, new_right, updates = slot_step(own_count, received, left_stats[0], right_stats[0])
    returned = lax.all_to_all(updates, "dp", split_axis=0, concat_axis=0, tiled=True)
    returned = returned.reshape(-1, *returned.shape[2:])
    slot_of_block = jnp.arange(blocks, dtype=jnp.int32) - offsets_row[owners_row]
    position = owners_row * slots + slot_of_block
    placed = [returned[position[: blocks // 2]], returned[position[blocks // 2 :]]]
    return new_left[None], new_right[None], gather_groups(placed, group, core)


def solution(mesh):
    placed = (
        P("dp", "mp", None, None, None),
        P("mp", "dp", None, None),
        P("mp", "dp", None, None),
        P(),
        P(),
        P(),
    )
    return jax.shard_map(
        per_device,
        mesh=mesh,
        in_specs=placed,
        out_specs=(P("mp", "dp", None, None), P("mp", "dp", None, None), P(None, None, "dp", None)),
        check_vma=False,
    )
```

```python
import functools

import jax
import jax.numpy as jnp
import numpy as np
from jax import lax
from jax.experimental import pallas as pl
from jax.experimental.pallas import tpu as pltpu
from jax.sharding import PartitionSpec as P

RING = 4
CORES = 2
START = 25.0 / 16.0
VMEM = 47 * 1024 * 1024
SETS = (10, 4)
PLACES = 2


def tail_coefficients():
    m1 = np.polynomial.Polynomial([1.25, -0.25])
    m2 = 1.25 - 0.25 * np.polynomial.Polynomial([0.0, 1.0]) * m1**4
    return [float(v) for v in (m1 * m2).coef]


TAIL = tail_coefficients()
EYE_PART = 1.25 * TAIL[0]


def dot(first, second, dims=((1,), (0,))):
    return lax.dot_general(
        first.astype(jnp.bfloat16),
        second.astype(jnp.bfloat16),
        (dims, ((), ())),
        preferred_element_type=jnp.float32,
    )


def mirrored(pair):
    top, low = (part.astype(jnp.bfloat16) for part in pair)
    half = low.shape[0]
    return jnp.concatenate([top, jnp.concatenate([top[:, half:].T, low], axis=1)], axis=0)


def product(first, second):
    half = first.shape[0] // 2
    return dot(first[:half], second), dot(first[half:], second[:, half:])


def mix(*terms):
    return tuple(sum(factor * pair[k] for factor, pair in terms) for k in (0, 1))


def roots(statistics):
    both = range(len(statistics))
    half = statistics[0].shape[0] // 2
    scales = [jnp.max(jnp.sum(jnp.abs(a), axis=0, keepdims=True), axis=1, keepdims=True) + 1e-06 for a in statistics]
    z = [tuple(v * (1.0 / scales[i]) for v in (statistics[i][:half], statistics[i][half:, half:])) for i in both]
    zb = [mirrored(z[i]) for i in both]
    square = [product(zb[i], zb[i]) for i in both]
    e = [mirrored(mix((0.0625, square[i]), (-0.625, z[i]))) for i in both]
    t = [mix((START, z[i]), (1.0, product(e[i], zb[i]))) for i in both]
    tb = [mirrored(t[i]) for i in both]
    y = [mix((START, t[i]), (1.0, product(e[i], tb[i]))) for i in both]
    yb = [mirrored(y[i]) for i in both]
    y2 = [product(yb[i], yb[i]) for i in both]
    y2b = [mirrored(y2[i]) for i in both]
    y3 = [product(y2b[i], yb[i]) for i in both]
    y3b = [mirrored(y3[i]) for i in both]
    high = [mirrored(mix((TAIL[6], y3[i]), (TAIL[5], y2[i]), (TAIL[4], y[i]))) for i in both]
    q = [mix((TAIL[1], y[i]), (TAIL[2], y2[i]), (TAIL[3], y3[i]), (1.0, product(high[i], y3b[i]))) for i in both]
    qb = [mirrored(q[i]) for i in both]
    f = [mirrored(mix((1.25, q[i]), (-0.25 * TAIL[0], z[i]), (-0.25, product(zb[i], qb[i])))) for i in both]
    return f, [1.0 / jnp.sqrt(jnp.sqrt(s)) for s in scales]


def slot_kernel(count_ref, block_ref, left_ref, right_ref, new_left_ref, new_right_ref, update_ref, held, sems):
    slot = pl.program_id(0)
    alive = slot < count_ref[0]
    extent = left_ref.shape[-1]
    outs = (new_left_ref, new_right_ref)

    @pl.when(jnp.logical_not(alive))
    def _():
        held[0] = left_ref[0]
        held[1] = right_ref[0]
        update_ref[...] = jnp.zeros_like(update_ref)

    @pl.when(alive)
    def _():
        block = block_ref[:, 0].reshape(extent, extent)
        low = pl.ds(extent // 2, extent // 2)
        top = pl.ds(0, extent // 2)
        rows, turned = block[: extent // 2], block[:, : extent // 2]
        held[0, top] = 0.9 * left_ref[0, top] + (0.1 / extent) * dot(rows, block, ((1,), (1,)))
        held[1, top] = 0.9 * right_ref[0, top] + (0.1 / extent) * dot(turned, block, ((0,), (0,)))
        rows, turned = block[extent // 2 :], block[:, extent // 2 :]
        held[0, low, low] = 0.9 * left_ref[0, low, low] + (0.1 / extent) * dot(rows, rows, ((1,), (1,)))
        held[1, low, low] = 0.9 * right_ref[0, low, low] + (0.1 / extent) * dot(turned, turned, ((0,), (0,)))
        held[0, low, top] = held[0, top, low].T
        held[1, low, top] = held[1, top, low].T

    stores = [pltpu.make_async_copy(held.at[k], outs[k].at[slot], sems.at[k]) for k in (0, 1)]
    for store in stores:
        store.start()

    @pl.when(alive)
    def _():
        block = block_ref[:, 0].reshape(extent, extent)
        (f_left, f_right), (c_left, c_right) = roots([held[0], held[1]])
        half = EYE_PART * block.astype(jnp.float32) + dot(block, f_right)
        result = (EYE_PART * half + dot(f_left, half)) * (c_left * c_right)
        update_ref[:, 0] = result.astype(jnp.bfloat16).reshape(update_ref.shape[0], update_ref.shape[2], extent)

    for store in stores:
        store.wait()


def slot_step(count, received, left, right):
    owners, slots, rows, extent = received.shape
    spread = pl.BlockSpec((owners, 1, rows, extent), lambda s, count: (0, s, 0, 0))
    whole = pl.BlockSpec((1, extent, extent), lambda s, count: (s, 0, 0))
    anywhere = pl.BlockSpec(memory_space=pl.ANY)
    return pl.pallas_call(
        slot_kernel,
        grid_spec=pltpu.PrefetchScalarGridSpec(
            num_scalar_prefetch=1,
            grid=(slots,),
            in_specs=[spread, whole, whole],
            out_specs=[anywhere, anywhere, spread],
            scratch_shapes=[pltpu.VMEM((2, extent, extent), jnp.float32), pltpu.SemaphoreType.DMA((2,))],
        ),
        out_shape=[
            jax.ShapeDtypeStruct(left.shape, jnp.float32),
            jax.ShapeDtypeStruct(right.shape, jnp.float32),
            jax.ShapeDtypeStruct(received.shape, jnp.bfloat16),
        ],
        compiler_params=pltpu.CompilerParams(vmem_limit_bytes=49 * 1024 * 1024),
        cost_estimate=pl.CostEstimate(
            flops=slots * 18 * 2 * extent**3,
            bytes_accessed=4 * left.size * 4 + 2 * received.size * 2,
            transcendentals=0,
        ),
    )(count, received, left, right)


def flat(z, y, core):
    return (z * RING + y) * CORES + core


def places():
    return [(z, y, core) for z in range(RING) for y in range(RING) for core in range(CORES)]


def partner(place, core, step):
    flipped = place + 1 - 2 * (place % 2)
    mirrored = RING - 1 - place
    late = core + step - 2 * core * step
    return flipped + late * (mirrored - flipped)


def chunk(place, core, which):
    return {
        0: place,
        1: partner(place, core, 0),
        2: partner(place, core, 1),
        3: (place + RING // 2) % RING,
    }[which]


def exchange(value, axis, step):
    pairs = []
    for z, y, core in places():
        to = (partner(z, core, step), y, core) if axis == 0 else (z, partner(y, core, step), core)
        pairs.append((flat(z, y, core), flat(*to)))
    return lax.ppermute(value, "dp", pairs)


def swap(value):
    return lax.ppermute(value, "dp", [(flat(z, y, core), flat(z, y, 1 - core)) for z, y, core in places()])


def cut_specs(shape, which, half, other=False):
    _, _, _, _, rows, extent = shape
    size = SETS[half]
    start = 2 * sum(SETS[:half]) // size

    def whose(pos):
        return 1 - pos[2] if other else pos[2]

    def first(i, pos):
        return (start, 0, chunk(pos[1], whose(pos), which), whose(pos), 0, 0)

    def second(i, pos):
        return (start + 1, chunk(pos[0], whose(pos), which), 0, whose(pos), 0, 0)

    return [
        pl.BlockSpec((size, RING, 1, 1, rows, extent), first),
        pl.BlockSpec((size, 1, RING, 1, rows, extent), second),
    ]


def local_call(body, pos, in_specs, args, out_specs, out_shape, scratch=(), steps=1):
    moved = sum(4 * v.size for v in out_shape)
    return pl.pallas_call(
        body,
        grid_spec=pltpu.PrefetchScalarGridSpec(
            num_scalar_prefetch=1,
            grid=(steps,),
            in_specs=in_specs,
            out_specs=out_specs,
            scratch_shapes=list(scratch),
        ),
        out_shape=out_shape,
        compiler_params=pltpu.CompilerParams(vmem_limit_bytes=VMEM),
        cost_estimate=pl.CostEstimate(flops=moved, bytes_accessed=2 * moved, transcendentals=0),
    )(pos, *args)


def cut_kernel(count, pos, *refs):
    ins, outs = refs[: 2 * count], refs[2 * count :]
    for k in range(count):
        for part in (0, 1):
            outs[part][k] = ins[2 * k + part][...].reshape(outs[part].shape[1:])


def cut(view, pos, which, half):
    rows, extent = view.shape[-2:]
    shape = (len(which), SETS[half], RING, rows, extent)
    specs = [spec for w in which for spec in cut_specs(view.shape, w, half, other=True)]
    return local_call(
        functools.partial(cut_kernel, len(which)),
        pos,
        specs,
        [view] * len(specs),
        [pl.BlockSpec(shape, lambda i, pos: (0, 0, 0, 0, 0))] * 2,
        [jax.ShapeDtypeStruct(shape, jnp.bfloat16)] * 2,
    )


def add_up(own_ref, part, others):
    value = (own_ref[:, :, 0, 0] if part == 0 else own_ref[:, 0, :, 0]).astype(jnp.float32)
    for other in others:
        value = value + other.astype(jnp.float32)
    return value


def first_kernel(pos, *refs):
    views, others, outs = refs[:4], refs[4:6], refs[6:]
    for part in (0, 1):
        for k in (0, 1):
            outs[part][k] = add_up(views[2 * k + part], part, [others[part][k]]).astype(jnp.bfloat16)


def first_sums(view, pos, half, others):
    whole = pl.BlockSpec(others[0].shape, lambda i, pos: (0, 0, 0, 0, 0))
    specs = [spec for w in (3, 1) for spec in cut_specs(view.shape, w, half)]
    shape = [jax.ShapeDtypeStruct(others[0].shape, jnp.bfloat16)] * 2
    return local_call(first_kernel, pos, specs + [whole] * 2, [view] * 4 + list(others), [whole] * 2, shape)


def second_kernel(pos, *refs):
    views, others, arrived, outs = refs[:2], refs[2:4], refs[4:6], refs[6:]
    for part in (0, 1):
        outs[part][...] = add_up(views[part], part, [others[part][0], arrived[part][0]]).astype(jnp.bfloat16)


def second_sums(view, pos, half, others, arrived):
    shape = others[0].shape[1:]
    lead = pl.BlockSpec((1, *shape), lambda i, pos: (0, 0, 0, 0, 0))
    whole = pl.BlockSpec(shape, lambda i, pos: (0, 0, 0, 0))
    specs = cut_specs(view.shape, 2, half) + [lead] * 4
    out = [jax.ShapeDtypeStruct(shape, jnp.bfloat16)] * 2
    return local_call(second_kernel, pos, specs, [view] * 2 + list(others) + list(arrived), [whole] * 2, out)


def rest_kernel(pos, *refs):
    views, others, direct, outs = refs[:2], refs[2:4], refs[4:6], refs[6:]
    for part in (0, 1):
        outs[part][...] = add_up(views[part], part, [others[part][0], direct[part][0]])


def rest_sums(view, pos, half, others, direct):
    shape = (SETS[half], RING, *view.shape[-2:])
    tail = pl.BlockSpec((1, *shape), lambda i, pos: (1, 0, 0, 0, 0))
    whole = pl.BlockSpec(shape, lambda i, pos: (0, 0, 0, 0))
    out = [jax.ShapeDtypeStruct(shape, jnp.float32)] * 2
    specs = cut_specs(view.shape, 0, half) + [tail] * 4
    return local_call(rest_kernel, pos, specs, [view] * 2 + [*others, *direct], [whole] * 2, out)


def last_kernel(pos, *refs):
    rest, joined = refs[:2], refs[2:4]
    filled, outs, scratch = refs[4:-7], refs[-7:-1], refs[-1]
    size = scratch.shape[0]
    start = outs[1].shape[0] - size
    for earlier, out_ref in zip(filled, outs):
        if len(earlier.shape) == 4:
            out_ref[:, pl.ds(0, start)] = earlier[...]
        else:
            out_ref[pl.ds(0, start)] = earlier[...]
    for part in (0, 1):
        ahead_ref, later_ref, own_ref = outs[3 * part : 3 * part + 3]
        scratch[...] = rest[part][...] + joined[part][...].astype(jnp.float32)
        place, core = pos[part], pos[2]
        here = pl.ds(start, size)
        for k, which in enumerate((3, 1)):
            ahead_ref[k, here] = scratch[:, chunk(place, core, which)].astype(jnp.bfloat16)
        later_ref[here] = scratch[:, chunk(place, core, 2)]
        own_ref[here] = scratch[:, place]


def last_sums(view, pos, half, rest, joined, filled):
    rows, extent = view.shape[-2:]
    shape = (SETS[half], RING, rows, extent)
    so_far = sum(SETS[: half + 1])
    whole = pl.BlockSpec(shape, lambda i, pos: (0, 0, 0, 0))

    def pieces(count):
        ahead = pl.BlockSpec((2, count, rows, extent), lambda i, pos: (0, 0, 0, 0))
        piece = pl.BlockSpec((count, rows, extent), lambda i, pos: (0, 0, 0))
        return [ahead, piece, piece] * 2

    return local_call(
        last_kernel,
        pos,
        [whole] * 4 + pieces(sum(SETS[:half]))[: len(filled)],
        [*rest, *joined, *filled],
        pieces(so_far),
        [
            jax.ShapeDtypeStruct((2, so_far, rows, extent), jnp.bfloat16),
            jax.ShapeDtypeStruct((so_far, rows, extent), jnp.float32),
            jax.ShapeDtypeStruct((so_far, rows, extent), jnp.float32),
        ]
        * 2,
        [pltpu.VMEM(shape, jnp.float32)],
    )


def reduce_scatter(gradient, pos):
    blocks, extent = gradient.shape[0], gradient.shape[1]
    rows = extent // (RING * RING * CORES)
    parts = (0, 1)
    halves = range(len(SETS))
    view = gradient.reshape(blocks, RING, RING, CORES, rows, extent)
    left, swapped = view, []

    def send_across(left, which, half):
        pieces = cut(left, pos, which, half)
        left, *pieces = lax.optimization_barrier((left, *pieces))
        return left, [swap(v) for v in pieces]

    for which, half in (((3, 1), 0), ((3, 1), 1), ((2, 0), 0)):
        left, values = send_across(left, which, half)
        swapped.append(values)
    direct = []
    for half in halves:
        sums = first_sums(left, pos, half, swapped[half])
        left, *sums = lax.optimization_barrier((left, *sums))
        direct.append([exchange(v, 1 - part, 0) for part, v in zip(parts, sums)])
    left, values = send_across(left, (2, 0), 1)
    late = [swapped[2], values]
    joined, terms, pieces = [], [], []
    for half in halves:
        sums = second_sums(left, pos, half, late[half], direct[half])
        if half + 1 < len(SETS):
            *sums, direct[half + 1][0] = lax.optimization_barrier((*sums, direct[half + 1][0]))
        joined.append([exchange(v, 1 - part, 1) for part, v in zip(parts, sums)])
    rest = [rest_sums(left, pos, half, late[half], direct[half]) for half in halves]
    for half in halves:
        pieces = last_sums(left, pos, half, rest[half], joined[half], pieces)
    for part in parts:
        ahead, later, own = pieces[3 * part : 3 * part + 3]
        arrived = exchange(ahead, part, 0)
        more = exchange((later + arrived[0].astype(jnp.float32)).astype(jnp.bfloat16), part, 1)
        terms += [own, arrived, more]
    return terms


def place_kernel(wanted, *refs):
    *terms, out_ref, summed = refs
    @pl.when(pl.program_id(0) == 0)
    def _():
        for part, (own, arrived, more) in enumerate(zip(terms[::3], terms[1::3], terms[2::3])):
            value = own[...] + arrived[0].astype(jnp.float32) + more[...].astype(jnp.float32)
            value = value.astype(jnp.bfloat16)
            for half, size in enumerate(SETS):
                start = sum(SETS[:half])
                summed[pl.ds(2 * start + part * size, size)] = value[start : start + size]

    first = pl.program_id(0) * out_ref.shape[0]

    def copy(i, carry):
        out_ref[i] = summed[wanted[first + i]]
        return carry

    lax.fori_loop(0, out_ref.shape[0], copy, 0)


def to_slots(terms, wanted):
    rows, extent = terms[0].shape[1:]
    shape = (wanted.shape[0], rows, extent)
    specs = []
    for own in terms[::3]:
        piece = pl.BlockSpec(own.shape, lambda i, wanted: (0, 0, 0))
        lead = pl.BlockSpec((1, *own.shape), lambda i, wanted: (1, 0, 0, 0))
        specs += [piece, lead, piece]
    (out,) = local_call(
        place_kernel,
        wanted,
        specs,
        terms,
        [pl.BlockSpec((shape[0] // PLACES, *shape[1:]), lambda i, wanted: (i, 0, 0))],
        [jax.ShapeDtypeStruct(shape, jnp.bfloat16)],
        [pltpu.VMEM((2 * sum(SETS), rows, extent), jnp.bfloat16)],
        PLACES,
    )
    return out


def send_group(value, steps):
    groups = lax.axis_size("mp")
    pairs = []
    for z, y, core in places():
        for group in range(groups):
            ahead = -steps if core else steps
            pairs.append((flat(z, y, core) * groups + group, flat(z, y, core) * groups + (group + ahead) % groups))
    return lax.ppermute(value, ("dp", "mp"), pairs)


def gather_groups(halves, group, core):
    groups = lax.axis_size("mp")
    sign = 1 - 2 * core
    size = halves[0].shape[0]
    behind = [send_group(v, 1) for v in halves]
    before = [send_group(v, -1) for v in halves]
    opposite = [send_group(v, 1) for v in behind]
    out = jnp.zeros((groups, size * len(halves), *halves[0].shape[1:]), halves[0].dtype)
    for away, values in ((0, halves), (-1, behind), (2, opposite), (1, before)):
        for k, value in enumerate(values):
            place = ((group + sign * away + groups) % groups, size * k, 0, 0)
            out = lax.dynamic_update_slice(out, value[None], place)
    return out


def per_device(gradients, left_stats, right_stats, owner_list, owner_counts, block_offsets):
    group = lax.axis_index("mp")
    owner = lax.axis_index("dp")
    blocks = gradients.shape[2]
    slots = left_stats.shape[1]
    core = owner % CORES
    y = (owner // CORES) % RING
    z = owner // (CORES * RING)
    counts_row = lax.dynamic_index_in_dim(owner_counts, group, 0, keepdims=False)
    offsets_row = lax.dynamic_index_in_dim(block_offsets, group, 0, keepdims=False)
    owners_row = lax.dynamic_index_in_dim(owner_list, group, 0, keepdims=False)
    slot_ids = jnp.arange(slots, dtype=jnp.int32)
    wanted = jnp.minimum(offsets_row[:, None] + slot_ids[None, :], blocks - 1)

    terms = reduce_scatter(gradients[0, 0], jnp.stack([z, y, core]).astype(jnp.int32))
    outgoing = to_slots(terms, wanted.reshape(-1)).reshape(-1, slots, *terms[0].shape[1:])
    received = lax.all_to_all(outgoing, "dp", split_axis=0, concat_axis=0, tiled=True)
    own_count = lax.dynamic_slice(counts_row, (owner,), (1,))
    new_left, new_right, updates = slot_step(own_count, received, left_stats[0], right_stats[0])
    returned = lax.all_to_all(updates, "dp", split_axis=0, concat_axis=0, tiled=True)
    returned = returned.reshape(-1, *returned.shape[2:])
    slot_of_block = jnp.arange(blocks, dtype=jnp.int32) - offsets_row[owners_row]
    position = owners_row * slots + slot_of_block
    placed = [returned[position[: blocks // 2]], returned[position[blocks // 2 :]]]
    return new_left[None], new_right[None], gather_groups(placed, group, core)


def solution(mesh):
    placed = (
        P("dp", "mp", None, None, None),
        P("mp", "dp", None, None),
        P("mp", "dp", None, None),
        P(),
        P(),
        P(),
    )
    return jax.shard_map(
        per_device,
        mesh=mesh,
        in_specs=placed,
        out_specs=(P("mp", "dp", None, None), P("mp", "dp", None, None), P(None, None, "dp", None)),
        check_vma=False,
    )
```

```python
import functools

import jax
import jax.numpy as jnp
import numpy as np
from jax import lax
from jax.experimental import pallas as pl
from jax.experimental.pallas import tpu as pltpu
from jax.sharding import PartitionSpec as P

RING = 4
CORES = 2
START = 25.0 / 16.0
VMEM = 47 * 1024 * 1024
SETS = (10, 4)
STEPS = 2
PLACES = 2


def tail_coefficients():
    m1 = np.polynomial.Polynomial([1.25, -0.25])
    m2 = 1.25 - 0.25 * np.polynomial.Polynomial([0.0, 1.0]) * m1**4
    return [float(v) for v in (m1 * m2).coef]


TAIL = tail_coefficients()
EYE_PART = 1.25 * TAIL[0]


def dot(first, second, dims=((1,), (0,))):
    return lax.dot_general(
        first.astype(jnp.bfloat16),
        second.astype(jnp.bfloat16),
        (dims, ((), ())),
        preferred_element_type=jnp.float32,
    )


def mirrored(pair):
    top, low = (part.astype(jnp.bfloat16) for part in pair)
    half = low.shape[0]
    return jnp.concatenate([top, jnp.concatenate([top[:, half:].T, low], axis=1)], axis=0)


def product(first, second):
    half = first.shape[0] // 2
    return dot(first[:half], second), dot(first[half:], second[:, half:])


def mix(*terms):
    return tuple(sum(factor * pair[k] for factor, pair in terms) for k in (0, 1))


def roots(statistics):
    both = range(len(statistics))
    half = statistics[0].shape[0] // 2
    scales = [jnp.max(jnp.sum(jnp.abs(a), axis=0, keepdims=True), axis=1, keepdims=True) + 1e-06 for a in statistics]
    z = [tuple(v * (1.0 / scales[i]) for v in (statistics[i][:half], statistics[i][half:, half:])) for i in both]
    zb = [mirrored(z[i]) for i in both]
    square = [product(zb[i], zb[i]) for i in both]
    e = [mirrored(mix((0.0625, square[i]), (-0.625, z[i]))) for i in both]
    t = [mix((START, z[i]), (1.0, product(e[i], zb[i]))) for i in both]
    tb = [mirrored(t[i]) for i in both]
    y = [mix((START, t[i]), (1.0, product(e[i], tb[i]))) for i in both]
    yb = [mirrored(y[i]) for i in both]
    y2 = [product(yb[i], yb[i]) for i in both]
    y2b = [mirrored(y2[i]) for i in both]
    y3 = [product(y2b[i], yb[i]) for i in both]
    y3b = [mirrored(y3[i]) for i in both]
    high = [mirrored(mix((TAIL[6], y3[i]), (TAIL[5], y2[i]), (TAIL[4], y[i]))) for i in both]
    q = [mix((TAIL[1], y[i]), (TAIL[2], y2[i]), (TAIL[3], y3[i]), (1.0, product(high[i], y3b[i]))) for i in both]
    qb = [mirrored(q[i]) for i in both]
    f = [mirrored(mix((1.25, q[i]), (-0.25 * TAIL[0], z[i]), (-0.25, product(zb[i], qb[i])))) for i in both]
    return f, [1.0 / jnp.sqrt(jnp.sqrt(s)) for s in scales]


def slot_kernel(count_ref, block_ref, left_ref, right_ref, new_left_ref, new_right_ref, update_ref, held, sems):
    slot = pl.program_id(0)
    alive = slot < count_ref[0]
    extent = left_ref.shape[-1]
    outs = (new_left_ref, new_right_ref)

    @pl.when(jnp.logical_not(alive))
    def _():
        held[0] = left_ref[0]
        held[1] = right_ref[0]
        update_ref[...] = jnp.zeros_like(update_ref)

    @pl.when(alive)
    def _():
        block = block_ref[:, 0].reshape(extent, extent)
        low = pl.ds(extent // 2, extent // 2)
        top = pl.ds(0, extent // 2)
        rows, turned = block[: extent // 2], block[:, : extent // 2]
        held[0, top] = 0.9 * left_ref[0, top] + (0.1 / extent) * dot(rows, block, ((1,), (1,)))
        held[1, top] = 0.9 * right_ref[0, top] + (0.1 / extent) * dot(turned, block, ((0,), (0,)))
        rows, turned = block[extent // 2 :], block[:, extent // 2 :]
        held[0, low, low] = 0.9 * left_ref[0, low, low] + (0.1 / extent) * dot(rows, rows, ((1,), (1,)))
        held[1, low, low] = 0.9 * right_ref[0, low, low] + (0.1 / extent) * dot(turned, turned, ((0,), (0,)))
        held[0, low, top] = held[0, top, low].T
        held[1, low, top] = held[1, top, low].T

    stores = [pltpu.make_async_copy(held.at[k], outs[k].at[slot], sems.at[k]) for k in (0, 1)]
    for store in stores:
        store.start()

    @pl.when(alive)
    def _():
        block = block_ref[:, 0].reshape(extent, extent)
        (f_left, f_right), (c_left, c_right) = roots([held[0], held[1]])
        half = EYE_PART * block.astype(jnp.float32) + dot(block, f_right)
        result = (EYE_PART * half + dot(f_left, half)) * (c_left * c_right)
        update_ref[:, 0] = result.astype(jnp.bfloat16).reshape(update_ref.shape[0], update_ref.shape[2], extent)

    for store in stores:
        store.wait()


def slot_step(count, received, left, right):
    owners, slots, rows, extent = received.shape
    spread = pl.BlockSpec((owners, 1, rows, extent), lambda s, count: (0, s, 0, 0))
    whole = pl.BlockSpec((1, extent, extent), lambda s, count: (s, 0, 0))
    anywhere = pl.BlockSpec(memory_space=pl.ANY)
    return pl.pallas_call(
        slot_kernel,
        grid_spec=pltpu.PrefetchScalarGridSpec(
            num_scalar_prefetch=1,
            grid=(slots,),
            in_specs=[spread, whole, whole],
            out_specs=[anywhere, anywhere, spread],
            scratch_shapes=[pltpu.VMEM((2, extent, extent), jnp.float32), pltpu.SemaphoreType.DMA((2,))],
        ),
        out_shape=[
            jax.ShapeDtypeStruct(left.shape, jnp.float32),
            jax.ShapeDtypeStruct(right.shape, jnp.float32),
            jax.ShapeDtypeStruct(received.shape, jnp.bfloat16),
        ],
        compiler_params=pltpu.CompilerParams(vmem_limit_bytes=49 * 1024 * 1024),
        cost_estimate=pl.CostEstimate(
            flops=slots * 18 * 2 * extent**3,
            bytes_accessed=4 * left.size * 4 + 2 * received.size * 2,
            transcendentals=0,
        ),
    )(count, received, left, right)


def flat(z, y, core):
    return (z * RING + y) * CORES + core


def places():
    return [(z, y, core) for z in range(RING) for y in range(RING) for core in range(CORES)]


def partner(place, core, step):
    flipped = place + 1 - 2 * (place % 2)
    mirrored = RING - 1 - place
    late = core + step - 2 * core * step
    return flipped + late * (mirrored - flipped)


def chunk(place, core, which):
    return {
        0: place,
        1: partner(place, core, 0),
        2: partner(place, core, 1),
        3: (place + RING // 2) % RING,
    }[which]


def exchange(value, axis, step):
    pairs = []
    for z, y, core in places():
        to = (partner(z, core, step), y, core) if axis == 0 else (z, partner(y, core, step), core)
        pairs.append((flat(z, y, core), flat(*to)))
    return lax.ppermute(value, "dp", pairs)


def swap(value):
    return lax.ppermute(value, "dp", [(flat(z, y, core), flat(z, y, 1 - core)) for z, y, core in places()])


def cut_specs(shape, which, half, other=False, steps=1):
    _, _, _, _, rows, extent = shape
    size = SETS[half] // steps
    start = 2 * sum(SETS[:half]) // size

    def whose(pos):
        return 1 - pos[2] if other else pos[2]

    def first(i, pos):
        return (start + i, 0, chunk(pos[1], whose(pos), which), whose(pos), 0, 0)

    def second(i, pos):
        return (start + steps + i, chunk(pos[0], whose(pos), which), 0, whose(pos), 0, 0)

    return [
        pl.BlockSpec((size, RING, 1, 1, rows, extent), first),
        pl.BlockSpec((size, 1, RING, 1, rows, extent), second),
    ]


def local_call(body, pos, in_specs, args, out_specs, out_shape, scratch=(), steps=1):
    moved = sum(4 * v.size for v in out_shape)
    return pl.pallas_call(
        body,
        grid_spec=pltpu.PrefetchScalarGridSpec(
            num_scalar_prefetch=1,
            grid=(steps,),
            in_specs=in_specs,
            out_specs=out_specs,
            scratch_shapes=list(scratch),
        ),
        out_shape=out_shape,
        compiler_params=pltpu.CompilerParams(vmem_limit_bytes=VMEM),
        cost_estimate=pl.CostEstimate(flops=moved, bytes_accessed=2 * moved, transcendentals=0),
    )(pos, *args)


def cut_kernel(count, pos, *refs):
    ins, outs = refs[: 2 * count], refs[2 * count :]
    for k in range(count):
        for part in (0, 1):
            outs[part][k] = ins[2 * k + part][...].reshape(outs[part].shape[1:])


def cut(view, pos, which, half):
    rows, extent = view.shape[-2:]
    shape = (len(which), SETS[half], RING, rows, extent)
    specs = [spec for w in which for spec in cut_specs(view.shape, w, half, other=True)]
    return local_call(
        functools.partial(cut_kernel, len(which)),
        pos,
        specs,
        [view] * len(specs),
        [pl.BlockSpec(shape, lambda i, pos: (0, 0, 0, 0, 0))] * 2,
        [jax.ShapeDtypeStruct(shape, jnp.bfloat16)] * 2,
    )


def add_up(own_ref, part, others):
    value = (own_ref[:, :, 0, 0] if part == 0 else own_ref[:, 0, :, 0]).astype(jnp.float32)
    for other in others:
        value = value + other.astype(jnp.float32)
    return value


def first_kernel(pos, *refs):
    views, others, outs = refs[:4], refs[4:6], refs[6:]
    for part in (0, 1):
        for k in (0, 1):
            outs[part][k] = add_up(views[2 * k + part], part, [others[part][k]]).astype(jnp.bfloat16)


def first_sums(view, pos, half, others):
    full = others[0].shape
    whole = pl.BlockSpec((full[0], full[1] // STEPS, *full[2:]), lambda i, pos: (0, i, 0, 0, 0))
    specs = [spec for w in (3, 1) for spec in cut_specs(view.shape, w, half, steps=STEPS)]
    shape = [jax.ShapeDtypeStruct(others[0].shape, jnp.bfloat16)] * 2
    return local_call(first_kernel, pos, specs + [whole] * 2, [view] * 4 + list(others), [whole] * 2, shape, steps=STEPS)


def second_kernel(pos, *refs):
    views, others, arrived, outs = refs[:2], refs[2:4], refs[4:6], refs[6:]
    for part in (0, 1):
        outs[part][...] = add_up(views[part], part, [others[part][0], arrived[part][0]]).astype(jnp.bfloat16)


def second_sums(view, pos, half, others, arrived):
    shape = others[0].shape[1:]
    lead = pl.BlockSpec((1, *shape), lambda i, pos: (0, 0, 0, 0, 0))
    whole = pl.BlockSpec(shape, lambda i, pos: (0, 0, 0, 0))
    specs = cut_specs(view.shape, 2, half) + [lead] * 4
    out = [jax.ShapeDtypeStruct(shape, jnp.bfloat16)] * 2
    return local_call(second_kernel, pos, specs, [view] * 2 + list(others) + list(arrived), [whole] * 2, out)


def rest_kernel(pos, *refs):
    views, others, direct, outs = refs[:2], refs[2:4], refs[4:6], refs[6:]
    for part in (0, 1):
        outs[part][...] = add_up(views[part], part, [others[part][0], direct[part][0]])


def rest_sums(view, pos, half, others, direct):
    shape = (SETS[half], RING, *view.shape[-2:])
    tail = pl.BlockSpec((1, *shape), lambda i, pos: (1, 0, 0, 0, 0))
    whole = pl.BlockSpec(shape, lambda i, pos: (0, 0, 0, 0))
    out = [jax.ShapeDtypeStruct(shape, jnp.float32)] * 2
    specs = cut_specs(view.shape, 0, half) + [tail] * 4
    return local_call(rest_kernel, pos, specs, [view] * 2 + [*others, *direct], [whole] * 2, out)


def last_kernel(pos, *refs):
    rest, joined = refs[:2], refs[2:4]
    filled, outs, scratch = refs[4:-7], refs[-7:-1], refs[-1]
    size = scratch.shape[0]
    start = outs[1].shape[0] - size
    for earlier, out_ref in zip(filled, outs):
        if len(earlier.shape) == 4:
            out_ref[:, pl.ds(0, start)] = earlier[...]
        else:
            out_ref[pl.ds(0, start)] = earlier[...]
    for part in (0, 1):
        ahead_ref, later_ref, own_ref = outs[3 * part : 3 * part + 3]
        scratch[...] = rest[part][...] + joined[part][...].astype(jnp.float32)
        place, core = pos[part], pos[2]
        here = pl.ds(start, size)
        for k, which in enumerate((3, 1)):
            ahead_ref[k, here] = scratch[:, chunk(place, core, which)].astype(jnp.bfloat16)
        later_ref[here] = scratch[:, chunk(place, core, 2)]
        own_ref[here] = scratch[:, place]


def last_sums(view, pos, half, rest, joined, filled):
    rows, extent = view.shape[-2:]
    shape = (SETS[half], RING, rows, extent)
    so_far = sum(SETS[: half + 1])
    whole = pl.BlockSpec(shape, lambda i, pos: (0, 0, 0, 0))

    def pieces(count):
        ahead = pl.BlockSpec((2, count, rows, extent), lambda i, pos: (0, 0, 0, 0))
        piece = pl.BlockSpec((count, rows, extent), lambda i, pos: (0, 0, 0))
        return [ahead, piece, piece] * 2

    return local_call(
        last_kernel,
        pos,
        [whole] * 4 + pieces(sum(SETS[:half]))[: len(filled)],
        [*rest, *joined, *filled],
        pieces(so_far),
        [
            jax.ShapeDtypeStruct((2, so_far, rows, extent), jnp.bfloat16),
            jax.ShapeDtypeStruct((so_far, rows, extent), jnp.float32),
            jax.ShapeDtypeStruct((so_far, rows, extent), jnp.float32),
        ]
        * 2,
        [pltpu.VMEM(shape, jnp.float32)],
    )


def reduce_scatter(gradient, pos):
    blocks, extent = gradient.shape[0], gradient.shape[1]
    rows = extent // (RING * RING * CORES)
    parts = (0, 1)
    halves = range(len(SETS))
    view = gradient.reshape(blocks, RING, RING, CORES, rows, extent)
    left, swapped = view, []

    def send_across(left, which, half):
        pieces = cut(left, pos, which, half)
        left, *pieces = lax.optimization_barrier((left, *pieces))
        return left, [swap(v) for v in pieces]

    for which, half in (((3, 1), 0), ((3, 1), 1), ((2, 0), 0)):
        left, values = send_across(left, which, half)
        swapped.append(values)
    direct = []
    for half in halves:
        sums = first_sums(left, pos, half, swapped[half])
        left, *sums = lax.optimization_barrier((left, *sums))
        direct.append([exchange(v, 1 - part, 0) for part, v in zip(parts, sums)])
    left, values = send_across(left, (2, 0), 1)
    late = [swapped[2], values]
    joined, terms, pieces = [], [], []
    for half in halves:
        sums = second_sums(left, pos, half, late[half], direct[half])
        if half + 1 < len(SETS):
            count = len(sums)
            both = lax.optimization_barrier((*sums, *direct[half + 1]))
            sums, direct[half + 1] = both[:count], both[count:]
        joined.append([exchange(v, 1 - part, 1) for part, v in zip(parts, sums)])
    rest = [rest_sums(left, pos, half, late[half], direct[half]) for half in halves]
    for half in halves:
        pieces = last_sums(left, pos, half, rest[half], joined[half], pieces)
    for part in parts:
        ahead, later, own = pieces[3 * part : 3 * part + 3]
        arrived = exchange(ahead, part, 0)
        more = exchange((later + arrived[0].astype(jnp.float32)).astype(jnp.bfloat16), part, 1)
        terms += [own, arrived, more]
    return terms


def place_kernel(wanted, *refs):
    *terms, out_ref, summed = refs
    @pl.when(pl.program_id(0) == 0)
    def _():
        for part, (own, arrived, more) in enumerate(zip(terms[::3], terms[1::3], terms[2::3])):
            value = own[...] + arrived[0].astype(jnp.float32) + more[...].astype(jnp.float32)
            value = value.astype(jnp.bfloat16)
            for half, size in enumerate(SETS):
                start = sum(SETS[:half])
                summed[pl.ds(2 * start + part * size, size)] = value[start : start + size]

    first = pl.program_id(0) * out_ref.shape[0]

    def copy(i, carry):
        out_ref[i] = summed[wanted[first + i]]
        return carry

    lax.fori_loop(0, out_ref.shape[0], copy, 0)


def to_slots(terms, wanted):
    rows, extent = terms[0].shape[1:]
    shape = (wanted.shape[0], rows, extent)
    specs = []
    for own in terms[::3]:
        piece = pl.BlockSpec(own.shape, lambda i, wanted: (0, 0, 0))
        lead = pl.BlockSpec((1, *own.shape), lambda i, wanted: (1, 0, 0, 0))
        specs += [piece, lead, piece]
    (out,) = local_call(
        place_kernel,
        wanted,
        specs,
        terms,
        [pl.BlockSpec((shape[0] // PLACES, *shape[1:]), lambda i, wanted: (i, 0, 0))],
        [jax.ShapeDtypeStruct(shape, jnp.bfloat16)],
        [pltpu.VMEM((2 * sum(SETS), rows, extent), jnp.bfloat16)],
        PLACES,
    )
    return out


def send_group(value, steps):
    groups = lax.axis_size("mp")
    pairs = []
    for z, y, core in places():
        for group in range(groups):
            ahead = -steps if core else steps
            pairs.append((flat(z, y, core) * groups + group, flat(z, y, core) * groups + (group + ahead) % groups))
    return lax.ppermute(value, ("dp", "mp"), pairs)


def gather_groups(halves, group, core):
    groups = lax.axis_size("mp")
    sign = 1 - 2 * core
    size = halves[0].shape[0]
    behind = [send_group(v, 1) for v in halves]
    before = [send_group(v, -1) for v in halves]
    opposite = [send_group(v, 1) for v in behind]
    out = jnp.zeros((groups, size * len(halves), *halves[0].shape[1:]), halves[0].dtype)
    for away, values in ((0, halves), (-1, behind), (2, opposite), (1, before)):
        for k, value in enumerate(values):
            place = ((group + sign * away + groups) % groups, size * k, 0, 0)
            out = lax.dynamic_update_slice(out, value[None], place)
    return out


def per_device(gradients, left_stats, right_stats, owner_list, owner_counts, block_offsets):
    group = lax.axis_index("mp")
    owner = lax.axis_index("dp")
    blocks = gradients.shape[2]
    slots = left_stats.shape[1]
    core = owner % CORES
    y = (owner // CORES) % RING
    z = owner // (CORES * RING)
    counts_row = lax.dynamic_index_in_dim(owner_counts, group, 0, keepdims=False)
    offsets_row = lax.dynamic_index_in_dim(block_offsets, group, 0, keepdims=False)
    owners_row = lax.dynamic_index_in_dim(owner_list, group, 0, keepdims=False)
    slot_ids = jnp.arange(slots, dtype=jnp.int32)
    wanted = jnp.minimum(offsets_row[:, None] + slot_ids[None, :], blocks - 1)

    terms = reduce_scatter(gradients[0, 0], jnp.stack([z, y, core]).astype(jnp.int32))
    outgoing = to_slots(terms, wanted.reshape(-1)).reshape(-1, slots, *terms[0].shape[1:])
    received = lax.all_to_all(outgoing, "dp", split_axis=0, concat_axis=0, tiled=True)
    own_count = lax.dynamic_slice(counts_row, (owner,), (1,))
    new_left, new_right, updates = slot_step(own_count, received, left_stats[0], right_stats[0])
    returned = lax.all_to_all(updates, "dp", split_axis=0, concat_axis=0, tiled=True)
    returned = returned.reshape(-1, *returned.shape[2:])
    slot_of_block = jnp.arange(blocks, dtype=jnp.int32) - offsets_row[owners_row]
    position = owners_row * slots + slot_of_block
    placed = [returned[position[: blocks // 2]], returned[position[blocks // 2 :]]]
    return new_left[None], new_right[None], gather_groups(placed, group, core)


def solution(mesh):
    placed = (
        P("dp", "mp", None, None, None),
        P("mp", "dp", None, None),
        P("mp", "dp", None, None),
        P(),
        P(),
        P(),
    )
    return jax.shard_map(
        per_device,
        mesh=mesh,
        in_specs=placed,
        out_specs=(P("mp", "dp", None, None), P("mp", "dp", None, None), P(None, None, "dp", None)),
        check_vma=False,
    )
```
